32 devices in a mesh: section: 4 (over x, core), ep: 8 (over z, y).
Axes of the slice: x: 2, y: 2, z: 4, core: 2. Of those that a mesh axis runs over, the one named last changes fastest.
Arguments:
- tokens: bfloat16 [2048, 1440], P('ep', 'section'), may hold values from -6 to 6
- grad_out: bfloat16 [2048, 1440], P('ep', 'section'), may hold values from -6 to 6
- expert_ids: int32 [2048, 4], P('ep'), may hold values from 0 to 7, all different within a row; in each aligned block of 256 rows (0 to 255, 256 to 511, ...) at most 192 rows name the same one
- probs: float32 [2048, 4], P('ep'), may hold values from 0.05 to 1
- w_gate: bfloat16 [8, 1440, 2880], P('ep', None, 'section'), may hold values from -0.15625 to 0.15625
- w_up: bfloat16 [8, 1440, 2880], P('ep', None, 'section'), may hold values from -0.15625 to 0.15625
- w_down: bfloat16 [8, 2880, 1440], P('ep', 'section'), may hold values from -0.109375 to 0.109375
Outputs:
- grad_gate: bfloat16 [8, 1440, 2880], P('ep', None, 'section')
- grad_up: bfloat16 [8, 1440, 2880], P('ep', None, 'section')
- grad_down: bfloat16 [8, 2880, 1440], P('ep', 'section')
The draws below stay inside these ranges and needn't reach their ends.
Inputs may be any that keep to these rules, and one draw needn't show every extreme that they name: `expert_ids`: among the picks of the 256 tokens of one index of ep, no expert is named more than 192 times, and the 4 experts of a token differ.
All inputs are finite; a program needn't handle non-finite values.
Results may differ from the reference program's by a relative error of at most 0.0065.
Values may be sent and summed in bfloat16 or wider, within the bound.
A program may use at most 128 MiB of HBM per device.

```python
import math
import jax
import jax.numpy as jnp
import numpy as np
from jax import lax

D = 1440
FF = 2880
TOP = 4
TOK_DEV = 256
EXPERTS = 8
TOKENS = 2048
CAP = 192
N_EP = 8


def block_scale(stream_key, extent, shards, smallest, high):
    def one(position, parts):
        steps = jax.random.uniform(jax.random.fold_in(jax.random.fold_in(stream_key, 6), position), (parts,), jnp.float32, smallest / len(shards), high / len(shards))
        return jnp.repeat(jnp.exp(steps), extent[position] // parts).reshape((-1,) + (1,) * (len(extent) - position - 1))

    level = one(*shards[0])
    for cut in shards[1:]:
        level = level * one(*cut)
    return level


def shared_out(rng, own, number, rows, amount, top, most, slope):
    order = jax.random.permutation(rng, amount)
    heavy_load, usual = load_shares(amount, rows * top, most, slope, True), load_shares(amount, rows * top, most, slope, False)
    places = jnp.arange(amount)

    def named(tallies, turn):
        used = int((tallies > 0).sum())
        fixed = max(1, used // 4)
        shifted = fixed + (places - fixed + turn * (used - fixed)) % max(1, amount - fixed)
        return jnp.zeros((amount,), jnp.int32).at[order[jnp.where(places < fixed, places, shifted)]].set(jnp.asarray(tallies, jnp.int32))

    tallies = jnp.where(number % 4 == 0, named(heavy_load, number // 4), named(usual, number - number // 4 - 1))
    mixed = jax.random.permutation(jax.random.fold_in(own, 3), amount)
    giver, taker = mixed[0:amount // 2 * 2:2], mixed[1:amount // 2 * 2:2]
    room = jnp.minimum(tallies[giver] - 1, most - tallies[taker]) // 2
    room = jnp.where((giver == order[0]) | (taker == order[0]) | (tallies[taker] == 0), 0, jnp.maximum(room, 0))
    shifted = jax.random.randint(jax.random.fold_in(own, 4), (amount // 2,), 0, 1 << 20) % (room + 1)
    tallies = tallies.at[giver].add(-shifted).at[taker].add(shifted)
    labels = jnp.searchsorted(jnp.cumsum(tallies), jnp.arange(rows * top), side="right").astype(jnp.int32)
    listing = labels.reshape(top, rows).T
    listing = listing[jax.random.permutation(jax.random.fold_in(own, 1), rows)]
    turn = jax.random.randint(jax.random.fold_in(own, 2), (rows, 1), 0, top)
    return jnp.take_along_axis(listing, (jnp.arange(top)[None, :] + turn) % top, axis=1)


def load_shares(count, total, most, lean, full):
    loads = [(1 << 20) // math.isqrt(standing ** lean) + 1 for standing in range(1, count + 1)]
    largest = most if full else min(most, max(-(-total // count), total * loads[0] // sum(loads)))
    least = 1 if total - largest >= count - 1 else 0
    holding, surplus = [largest] + [least] * (count - 1), total - largest - least * (count - 1)
    while surplus > 0:
        movable = [i for i in range(1, count) if holding[i] < largest] or [i for i in range(1, count) if holding[i] < most]
        mass, remaining = sum([loads[i] for i in movable]), surplus
        for i in movable:
            extra = min(most - holding[i], max(1, remaining * loads[i] // mass), surplus)
            holding[i] = holding[i] + extra
            surplus = surplus - extra
    return np.array(holding)


def noise(own_key, extent, deviation, reach, split=(), kind=jnp.bfloat16):
    array = jax.random.normal(own_key, extent, jnp.float32) * deviation
    if len(split) > 0:
        array = block_scale(own_key, extent, split, -0.22, 0.18) * array
    return jnp.clip(array, min=-reach, max=reach).astype(kind)


def setup_inputs(seed: int = 0) -> dict:
    keys = jax.random.split(jax.random.key(seed), 8)
    tokens = noise(keys[0], (TOKENS, D), 1.0, 6.0, ((0, 8), (1, 4)))
    grad_out = noise(keys[1], (TOKENS, D), 1.0, 6.0, ((0, 8), (1, 4)))
    expert_ids_keys = jax.random.split(jax.random.fold_in(keys[2], 1), TOKENS // TOK_DEV)
    expert_ids_turns = jax.random.permutation(jax.random.fold_in(keys[2], 3), TOKENS // TOK_DEV)
    expert_ids = jax.vmap(lambda own, number: shared_out(jax.random.fold_in(keys[2], 2), own, number, TOK_DEV, EXPERTS, TOP, CAP, 2))(expert_ids_keys, expert_ids_turns).reshape((TOKENS, TOP))
    probs = jnp.clip(jnp.exp(math.log(1.0) - 2.9957323 * jax.random.uniform(keys[3], (TOKENS, TOP), jnp.float32) ** block_scale(keys[3], (TOKENS, TOP), ((0, 8),), -0.2, 0.2)), 0.05, 1.0)
    w_gate = noise(keys[4], (EXPERTS, D, FF), D ** -0.5, 0.15625, ((0, 8), (2, 4)))
    w_up = noise(keys[5], (EXPERTS, D, FF), D ** -0.5, 0.15625, ((0, 8), (2, 4)))
    w_down = noise(keys[6], (EXPERTS, FF, D), FF ** -0.5, 0.109375, ((0, 8), (1, 4)))
    return {"tokens": tokens, "grad_out": grad_out, "expert_ids": expert_ids, "probs": probs, "w_gate": w_gate, "w_up": w_up, "w_down": w_down}


def rounded(value):
    return lax.optimization_barrier(value.astype(jnp.bfloat16)).astype(jnp.float32)


def reference(tokens, grad_out, expert_ids, probs, w_gate, w_up, w_down):
    picks = TOKENS * TOP
    flat_ids = expert_ids.reshape(picks).astype(jnp.int32)
    flat_probs = probs.reshape(picks)
    order = jnp.argsort(flat_ids, stable=True).astype(jnp.int32)
    counts = jnp.sum((flat_ids[:, None] == jnp.arange(EXPERTS, dtype=jnp.int32)[None, :]).astype(jnp.int32), axis=0)
    starts = (jnp.cumsum(counts) - counts).astype(jnp.int32)
    most_rows = N_EP * CAP
    slot_rows = jnp.arange(most_rows, dtype=jnp.int32)

    def one_expert(items):
        expert, gate_w, up_w, down_w = items
        start = starts[expert]
        count = counts[expert]
        where_pick = order[jnp.clip(start + slot_rows, 0, picks - 1)]
        valid = slot_rows < count
        token_row = (where_pick // TOP).astype(jnp.int32)
        inputs = tokens[token_row] * valid[:, None].astype(jnp.bfloat16)
        weight = jnp.where(valid, flat_probs[where_pick], 0.0)
        scaled = (weight[:, None] * grad_out[token_row].astype(jnp.float32)).astype(jnp.bfloat16)
        gate = jnp.dot(inputs, gate_w, preferred_element_type=jnp.float32)
        linear = jnp.dot(inputs, up_w, preferred_element_type=jnp.float32)
        sigma = jax.nn.sigmoid(gate)
        hidden = (gate * sigma * linear).astype(jnp.bfloat16)
        grad_hidden = jnp.dot(scaled, down_w.T, preferred_element_type=jnp.float32)
        gate_term = (grad_hidden * linear * sigma * (1.0 + gate * (1.0 - sigma))).astype(jnp.bfloat16)
        linear_term = (grad_hidden * gate * sigma).astype(jnp.bfloat16)
        lower = valid & (token_row < TOKENS // 2)
        upper = valid & (token_row >= TOKENS // 2)
        totals = []
        for mask in (lower, upper):
            weight_mask = mask[:, None].astype(jnp.bfloat16)
            masked_in = inputs * weight_mask
            masked_hidden = hidden * weight_mask
            part_gate = rounded(jnp.dot(masked_in.T, gate_term, preferred_element_type=jnp.float32))
            part_up = rounded(jnp.dot(masked_in.T, linear_term, preferred_element_type=jnp.float32))
            part_down = rounded(jnp.dot(masked_hidden.T, scaled, preferred_element_type=jnp.float32))
            totals.append((part_gate, part_up, part_down))
        return ((totals[0][0] + totals[1][0]).astype(jnp.bfloat16),
                (totals[0][1] + totals[1][1]).astype(jnp.bfloat16),
                (totals[0][2] + totals[1][2]).astype(jnp.bfloat16))

    grad_gate, grad_up, grad_down = lax.map(one_expert, (jnp.arange(EXPERTS, dtype=jnp.int32), w_gate, w_up, w_down))
    return grad_gate, grad_up, grad_down
```

```python
import jax
import jax.numpy as jnp
from jax import lax
from jax.experimental import pallas as pl
from jax.experimental.pallas import tpu as pltpu
from jax.sharding import PartitionSpec as P


def rounded(value):
    return lax.optimization_barrier(value.astype(jnp.bfloat16)).astype(jnp.float32)


def slot_grads(inputs, scaled, gate_w, up_w, down_w):
    gate = jnp.einsum("hpscd,sdf->hpscf", inputs, gate_w, preferred_element_type=jnp.float32)
    linear = jnp.einsum("hpscd,sdf->hpscf", inputs, up_w, preferred_element_type=jnp.float32)
    sigma = jax.nn.sigmoid(gate)
    hidden = (gate * sigma * linear).astype(jnp.bfloat16)
    grad_hidden = jnp.einsum("hpscd,sfd->hpscf", scaled, down_w, preferred_element_type=jnp.float32)
    gate_term = (grad_hidden * linear * sigma * (1.0 + gate * (1.0 - sigma))).astype(jnp.bfloat16)
    linear_term = (grad_hidden * gate * sigma).astype(jnp.bfloat16)
    part_gate = rounded(
        jnp.einsum("hpscd,hpscf->hsdf", inputs, gate_term, preferred_element_type=jnp.float32)
    )
    part_up = rounded(
        jnp.einsum("hpscd,hpscf->hsdf", inputs, linear_term, preferred_element_type=jnp.float32)
    )
    part_down = rounded(
        jnp.einsum("hpscf,hpscd->hsfd", hidden, scaled, preferred_element_type=jnp.float32)
    )
    return (part_gate, part_up, part_down)


def shards(tokens, grad_out, expert_ids, probs, w_gate, w_up, w_down):
    n_ep = lax.axis_size("ep")
    half = n_ep // 2
    tok_dev, top = expert_ids.shape
    picks = tok_dev * top
    capacity = max(2, (3 * picks + 2 * n_ep - 1) // (2 * n_ep))
    flat_ids = expert_ids.reshape(picks)
    owners = jnp.arange(n_ep, dtype=jnp.int32)
    slots = 1
    matches = (flat_ids[:, None] == owners[None, :]).astype(jnp.int32)
    rank = jnp.sum(jnp.cumsum(matches, axis=0) * matches, axis=1) - 1
    position = flat_ids * slots * capacity + rank
    width = tokens.shape[1]
    rows = jnp.repeat(tokens, top, axis=0)
    scaled = (
        probs.reshape(picks, 1) * jnp.repeat(grad_out, top, axis=0).astype(jnp.float32)
    ).astype(jnp.bfloat16)
    buffer_rows = n_ep * slots * capacity
    send_rows = jnp.zeros((buffer_rows, width), jnp.bfloat16).at[position].set(rows)
    send_scaled = jnp.zeros((buffer_rows, width), jnp.bfloat16).at[position].set(scaled)
    send_rows = send_rows.reshape(n_ep, slots * capacity, width)
    send_scaled = send_scaled.reshape(n_ep, slots * capacity, width)
    got_rows, got_scaled = (
        lax.all_to_all(send_rows, "ep", split_axis=0, concat_axis=0, tiled=True),
        lax.all_to_all(send_scaled, "ep", split_axis=0, concat_axis=0, tiled=True),
    )
    got_rows = got_rows.reshape(2, half, slots, capacity, width)
    got_scaled = got_scaled.reshape(2, half, slots, capacity, width)
    inputs, scaled_rows = (
        lax.all_gather(got_rows, "section", axis=4, tiled=True),
        lax.all_gather(got_scaled, "section", axis=4, tiled=True),
    )
    part_gate, part_up, part_down = slot_grads(inputs, scaled_rows, w_gate, w_up, w_down)
    grad_gate = (part_gate[0] + part_gate[1]).astype(jnp.bfloat16)
    grad_up = (part_up[0] + part_up[1]).astype(jnp.bfloat16)
    grad_down = (part_down[0] + part_down[1]).astype(jnp.bfloat16)
    return (grad_gate, grad_up, grad_down)


MESH = pl.DeviceIdType.MESH
TILE = 256


def fused_kernel(
    tokens, grad_out, ids, probs, w_gate, w_up, w_down,
    out_gate, out_up, out_down,
    held, wg, wu, wd, acc_gate, acc_up, acc_down, rows_in, rows_scaled, term_gate, term_linear, term_hidden,
    w_sem, z_send, z_recv, x_send, x_recv, y_send, y_recv, dx_send, dx_recv, dy_send, dy_recv, c_send, c_recv,
):
    sec, me = lax.axis_index("section"), lax.axis_index("ep")
    n_tok, width = tokens.shape
    wide = held.shape[-1]
    n_sec = held.shape[1]
    feats, units = w_gate.shape
    z, y = me // 2, me % 2
    h = z // 2
    zz = z + h * (3 - 2 * z)
    x_peer = (sec + 2) % 4
    core_peer = sec + 1 - 2 * (sec % 2)
    y_peer = me + 1 - 2 * y
    inward = me + 2 - 4 * h
    outward = me - 2 + 4 * h
    split = n_tok // 2

    loads = [
        pltpu.make_async_copy(src, dst, w_sem.at[i])
        for i, (src, dst) in enumerate(((w_gate, wg), (w_up, wu), (w_down, wd)))
    ]
    for load in loads:
        load.start()

    barrier = pltpu.get_barrier_semaphore()

    def greet(**where):
        pl.semaphore_signal(barrier, inc=1, device_id=where, device_id_type=MESH)

    greet(section=x_peer)
    greet(section=core_peer)
    greet(ep=y_peer)
    greet(ep=inward)

    @pl.when(zz == 1)
    def _():
        greet(ep=outward)

    own = held.at[me, sec]
    own[0, :, :width] = tokens[...]
    edge = wide - 128
    own[1, :, edge:] = jnp.zeros((n_tok, 128), jnp.bfloat16)
    own[1, :, :width] = grad_out[...]
    lane = lax.broadcasted_iota(jnp.int32, (n_tok, 128), 1)
    first = width - edge
    weight = jnp.zeros((n_tok, 128), jnp.float32)
    for k in range(ids.shape[1]):
        weight = weight + jnp.where(ids[:, k : k + 1] == lane % 8, probs[:, k : k + 1], 0.0)
    high = weight.astype(jnp.bfloat16).astype(jnp.float32)
    mid = (weight - high).astype(jnp.bfloat16).astype(jnp.float32)
    low = weight - high - mid
    parts = jnp.where(lane < first + 8, high, jnp.where(lane < first + 16, mid, low))
    last = own[1, :, edge:].astype(jnp.float32)
    own[1, :, edge:] = jnp.where(lane < first, last, parts).astype(jnp.bfloat16)

    @pl.when(zz == 0)
    def _():
        pl.semaphore_wait(barrier, 4)

    @pl.when(zz == 1)
    def _():
        pl.semaphore_wait(barrier, 5)

    def send(block, send_sem, recv_sem, **where):
        return pltpu.make_async_remote_copy(
            src_ref=block, dst_ref=block, send_sem=send_sem, recv_sem=recv_sem,
            device_id=where, device_id_type=MESH,
        )

    def source(k):
        s = k + (1 - k // 2) * ((k + zz) % 2 - k % 2)
        return s + h * (3 - 2 * s)

    def mine(k):
        return 2 * source(k) + y

    def other(k):
        return 2 * source(k) + 1 - y

    def upper(block):
        return block.at[:, :split]

    def lower(block):
        return block.at[:, split:]

    def z_in(k, idx):
        return send(held.at[mine(k), sec], z_send.at[0, idx], z_recv.at[idx], ep=inward)

    def z_out(k, idx):
        return send(held.at[mine(k), sec], z_send.at[1, idx], z_recv.at[idx], ep=outward)

    def x_whole(k):
        return send(held.at[mine(k), sec], x_send.at[k], x_recv.at[k], section=x_peer)

    def y_whole(k):
        return send(held.at[mine(k), sec], y_send.at[k], y_recv.at[k], ep=y_peer)

    def x_half(k):
        return send(upper(held.at[other(k), sec]), dx_send.at[k], dx_recv.at[k], section=x_peer)

    def y_half(k):
        return send(lower(held.at[mine(k), x_peer]), dy_send.at[k], dy_recv.at[k], ep=y_peer)

    def core(k, which):
        block = held.at[mine(k) if which < 2 else other(k), sec if which % 2 == 0 else x_peer]
        return send(block, c_send.at[k, which], c_recv.at[k, which], section=core_peer)

    def x_arrived(k):
        send(held.at[mine(k), x_peer], x_send.at[k], x_recv.at[k], section=x_peer).wait_recv()

    def y_arrived(k):
        send(held.at[other(k), sec], y_send.at[k], y_recv.at[k], ep=y_peer).wait_recv()

    def diagonal_arrived(k):
        block = held.at[other(k), x_peer]
        send(upper(block), dx_send.at[k], dx_recv.at[k], section=x_peer).wait_recv()
        send(lower(block), dy_send.at[k], dy_recv.at[k], ep=y_peer).wait_recv()

    def core_arrived(k, which):
        block = held.at[
            mine(k) if which < 2 else other(k),
            core_peer if which % 2 == 0 else (core_peer + 2) % 4,
        ]
        send(block, c_send.at[k, which], c_recv.at[k, which], section=core_peer).wait_recv()

    def column(k):
        x_whole(k).start()
        y_whole(k).start()
        core(k, 0).start()

    def forward(slot, row):
        here = pl.ds(row, n_tok)
        block = held.at[slot]
        rows_in[here, :feats] = jnp.concatenate([block[s, 0, :, :width] for s in range(n_sec)], axis=1)
        last = block[0, 1, :, edge:].astype(jnp.float32)
        weight = jnp.sum(jnp.where((lane >= first) & (lane % 8 == me), last, 0.0), axis=1, keepdims=True)
        cot = jnp.concatenate([block[s, 1, :, :width] for s in range(n_sec)], axis=1)
        rows_scaled[here, :] = (weight * cot.astype(jnp.float32)).astype(jnp.bfloat16)
        for at in range(0, units, TILE):
            to = min(units, at + TILE)
            gate = jnp.dot(rows_in[here, :feats], wg[:, at:to], preferred_element_type=jnp.float32)
            linear = jnp.dot(rows_in[here, :feats], wu[:, at:to], preferred_element_type=jnp.float32)
            grad = lax.dot_general(
                rows_scaled[here, :], wd[at:to, :], (((1,), (1,)), ((), ())),
                preferred_element_type=jnp.float32,
            )
            sigma = jax.nn.sigmoid(gate)
            silu = gate * sigma
            term_hidden[here, at:to] = (silu * linear).astype(jnp.bfloat16)
            term_gate[here, at:to] = (grad * linear * sigma * (1.0 + gate * (1.0 - sigma))).astype(jnp.bfloat16)
            term_linear[here, at:to] = (grad * silu).astype(jnp.bfloat16)

    def outer(lhs, rhs):
        return lax.dot_general(lhs, rhs, (((0,), (0,)), ((), ())), preferred_element_type=jnp.float32)

    def weights():
        def in_tile(m, carry):
            cols = pl.ds(pl.multiple_of(m * TILE, TILE), TILE)
            acc_gate[cols, :] += outer(rows_in[:, cols], term_gate[...])
            acc_up[cols, :] += outer(rows_in[:, cols], term_linear[...])
            return carry

        lax.fori_loop(0, rows_in.shape[1] // TILE, in_tile, 0)

        def hidden_tile(m, carry):
            cols = pl.ds(pl.multiple_of(m * TILE, TILE), TILE)
            acc_down[cols, :] += outer(term_hidden[:, cols], rows_scaled[...])
            return carry

        lax.fori_loop(0, term_hidden.shape[1] // TILE, hidden_tile, 0)

    z_in(0, 1 + zz).start()

    @pl.when(zz == 1)
    def _():
        z_out(0, 1).start()

    column(0)

    def clear(m, carry):
        cols = pl.ds(pl.multiple_of(m * TILE, TILE), TILE)
        acc_gate[cols, :] = jnp.zeros((TILE, units), jnp.float32)
        acc_up[cols, :] = jnp.zeros((TILE, units), jnp.float32)
        return carry

    lax.fori_loop(0, acc_gate.shape[0] // TILE, clear, 0)

    def clear_down(m, carry):
        cols = pl.ds(pl.multiple_of(m * TILE, TILE), TILE)
        acc_down[cols, :] = jnp.zeros((TILE, feats), jnp.float32)
        return carry

    lax.fori_loop(0, acc_down.shape[0] // TILE, clear_down, 0)

    for load in loads:
        load.wait()

    def step(k, carry):
        x_arrived(k)
        y_half(k).start()
        core(k, 1).start()
        y_arrived(k)
        x_half(k).start()
        core(k, 2).start()

        @pl.when(k < 3)
        def _():
            nxt = k + 1
            send(held.at[mine(nxt), sec], z_send.at[0, nxt], z_recv.at[nxt], ep=inward).wait_recv()

            @pl.when((zz == 1) & (nxt == 1))
            def _():
                z_in(nxt, 3).start()

            @pl.when((zz == 1) & (nxt >= 2))
            def _():
                z_out(nxt, nxt).start()

            column(nxt)

        core_arrived(k, 0)
        core_arrived(k, 1)
        forward(mine(k), 0)
        diagonal_arrived(k)
        core(k, 3).start()
        core_arrived(k, 2)
        core_arrived(k, 3)
        forward(other(k), n_tok)
        weights()
        return carry

    lax.fori_loop(0, 4, step, 0)

    def finish(m, carry):
        part = feats // 6
        here = pl.ds(pl.multiple_of(m * part, 16), part)
        out_gate[here, :] = acc_gate[here, :].astype(jnp.bfloat16)
        out_up[here, :] = acc_up[here, :].astype(jnp.bfloat16)
        return carry

    lax.fori_loop(0, 6, finish, 0)

    def finish_down(m, carry):
        part = units // 3
        here = pl.ds(pl.multiple_of(m * part, 16), part)
        out_down[here, :] = acc_down[here, :].astype(jnp.bfloat16)
        return carry

    lax.fori_loop(0, 3, finish_down, 0)

    z_in(0, 1 + zz).wait_send()

    @pl.when(zz == 1)
    def _():
        z_out(0, 1).wait_send()
        z_in(1, 3).wait_send()
        z_out(2, 2).wait_send()
        z_out(3, 3).wait_send()

    def drain(k, carry):
        x_whole(k).wait_send()
        y_whole(k).wait_send()
        x_half(k).wait_send()
        y_half(k).wait_send()
        for which in range(4):
            core(k, which).wait_send()
        return carry

    lax.fori_loop(0, 4, drain, 0)


def fused(tokens, grad_out, expert_ids, probs, w_gate, w_up, w_down):
    n_ep, n_sec = lax.axis_size("ep"), lax.axis_size("section")
    n_tok, width = tokens.shape
    feats, units = w_gate.shape[1:]
    wide = -(-(width + 3 * n_ep) // 128) * 128
    pad = lambda size: -(-size // TILE) * TILE
    bf16, f32 = jnp.bfloat16, jnp.float32
    dma = pltpu.SemaphoreType.DMA
    vmem, hbm = pl.BlockSpec(memory_space=pltpu.VMEM), pl.BlockSpec(memory_space=pl.ANY)
    rows = n_ep * n_tok
    outs = pl.pallas_call(
        fused_kernel,
        out_shape=(
            jax.ShapeDtypeStruct((feats, units), bf16),
            jax.ShapeDtypeStruct((feats, units), bf16),
            jax.ShapeDtypeStruct((units, feats), bf16),
        ),
        in_specs=[vmem] * 4 + [hbm] * 3,
        out_specs=(vmem,) * 3,
        scratch_shapes=[
            pltpu.VMEM((n_ep, n_sec, 2, n_tok, wide), bf16),
            pltpu.VMEM((feats, units), bf16),
            pltpu.VMEM((feats, units), bf16),
            pltpu.VMEM((units, feats), bf16),
            pltpu.VMEM((pad(feats), units), f32),
            pltpu.VMEM((pad(feats), units), f32),
            pltpu.VMEM((pad(units), feats), f32),
            pltpu.VMEM((2 * n_tok, pad(feats)), bf16),
            pltpu.VMEM((2 * n_tok, feats), bf16),
            pltpu.VMEM((2 * n_tok, units), bf16),
            pltpu.VMEM((2 * n_tok, units), bf16),
            pltpu.VMEM((2 * n_tok, pad(units)), bf16),
            dma((3,)),
            dma((2, 4)), dma((4,)),
            dma((4,)), dma((4,)), dma((4,)), dma((4,)),
            dma((4,)), dma((4,)), dma((4,)), dma((4,)),
            dma((4, 4)), dma((4, 4)),
        ],
        cost_estimate=pl.CostEstimate(
            flops=12 * rows * feats * units, bytes_accessed=12 * feats * units, transcendentals=rows * units
        ),
        compiler_params=pltpu.CompilerParams(
            collective_id=0, has_side_effects=True, vmem_limit_bytes=60 * 1024 * 1024
        ),
    )(tokens, grad_out, expert_ids, probs, w_gate[0], w_up[0], w_down[0])
    return tuple(out[None] for out in outs)


def solution(mesh):
    body = shards
    if mesh.shape["ep"] == 8 and mesh.shape["section"] == 4:
        body = fused
    placed = (
        P("ep", "section"),
        P("ep", "section"),
        P("ep", None),
        P("ep", None),
        P("ep", None, "section"),
        P("ep", None, "section"),
        P("ep", "section", None),
    )
    return jax.shard_map(
        body,
        mesh=mesh,
        in_specs=placed,
        out_specs=(P("ep", None, "section"), P("ep", None, "section"), P("ep", "section", None)),
        check_vma=False,
    )
```

```python
import jax
import jax.numpy as jnp
from jax import lax
from jax.experimental import pallas as pl
from jax.experimental.pallas import tpu as pltpu
from jax.sharding import PartitionSpec as P


def rounded(value):
    return lax.optimization_barrier(value.astype(jnp.bfloat16)).astype(jnp.float32)


def slot_grads(inputs, scaled, gate_w, up_w, down_w):
    gate = jnp.einsum("hpscd,sdf->hpscf", inputs, gate_w, preferred_element_type=jnp.float32)
    linear = jnp.einsum("hpscd,sdf->hpscf", inputs, up_w, preferred_element_type=jnp.float32)
    sigma = jax.nn.sigmoid(gate)
    hidden = (gate * sigma * linear).astype(jnp.bfloat16)
    grad_hidden = jnp.einsum("hpscd,sfd->hpscf", scaled, down_w, preferred_element_type=jnp.float32)
    gate_term = (grad_hidden * linear * sigma * (1.0 + gate * (1.0 - sigma))).astype(jnp.bfloat16)
    linear_term = (grad_hidden * gate * sigma).astype(jnp.bfloat16)
    part_gate = rounded(
        jnp.einsum("hpscd,hpscf->hsdf", inputs, gate_term, preferred_element_type=jnp.float32)
    )
    part_up = rounded(
        jnp.einsum("hpscd,hpscf->hsdf", inputs, linear_term, preferred_element_type=jnp.float32)
    )
    part_down = rounded(
        jnp.einsum("hpscf,hpscd->hsfd", hidden, scaled, preferred_element_type=jnp.float32)
    )
    return (part_gate, part_up, part_down)


def shards(tokens, grad_out, expert_ids, probs, w_gate, w_up, w_down):
    n_ep = lax.axis_size("ep")
    half = n_ep // 2
    tok_dev, top = expert_ids.shape
    picks = tok_dev * top
    capacity = max(2, (3 * picks + 2 * n_ep - 1) // (2 * n_ep))
    flat_ids = expert_ids.reshape(picks)
    owners = jnp.arange(n_ep, dtype=jnp.int32)
    slots = 1
    matches = (flat_ids[:, None] == owners[None, :]).astype(jnp.int32)
    rank = jnp.sum(jnp.cumsum(matches, axis=0) * matches, axis=1) - 1
    position = flat_ids * slots * capacity + rank
    width = tokens.shape[1]
    rows = jnp.repeat(tokens, top, axis=0)
    scaled = (
        probs.reshape(picks, 1) * jnp.repeat(grad_out, top, axis=0).astype(jnp.float32)
    ).astype(jnp.bfloat16)
    buffer_rows = n_ep * slots * capacity
    send_rows = jnp.zeros((buffer_rows, width), jnp.bfloat16).at[position].set(rows)
    send_scaled = jnp.zeros((buffer_rows, width), jnp.bfloat16).at[position].set(scaled)
    send_rows = send_rows.reshape(n_ep, slots * capacity, width)
    send_scaled = send_scaled.reshape(n_ep, slots * capacity, width)
    got_rows, got_scaled = (
        lax.all_to_all(send_rows, "ep", split_axis=0, concat_axis=0, tiled=True),
        lax.all_to_all(send_scaled, "ep", split_axis=0, concat_axis=0, tiled=True),
    )
    got_rows = got_rows.reshape(2, half, slots, capacity, width)
    got_scaled = got_scaled.reshape(2, half, slots, capacity, width)
    inputs, scaled_rows = (
        lax.all_gather(got_rows, "section", axis=4, tiled=True),
        lax.all_gather(got_scaled, "section", axis=4, tiled=True),
    )
    part_gate, part_up, part_down = slot_grads(inputs, scaled_rows, w_gate, w_up, w_down)
    grad_gate = (part_gate[0] + part_gate[1]).astype(jnp.bfloat16)
    grad_up = (part_up[0] + part_up[1]).astype(jnp.bfloat16)
    grad_down = (part_down[0] + part_down[1]).astype(jnp.bfloat16)
    return (grad_gate, grad_up, grad_down)


MESH = pl.DeviceIdType.MESH
TILE = 256


def fused_kernel(
    tokens, grad_out, ids, probs, w_gate, w_up, w_down,
    out_gate, out_up, out_down,
    held, wg, wu, wd, wg_t, wu_t, acc_gate, acc_up, acc_down, cols_in, cols_scaled, term_gate, term_linear, term_hidden,
    w_sem, z_send, z_recv, x_send, x_recv, y_send, y_recv, dx_send, dx_recv, dy_send, dy_recv, c_send, c_recv,
):
    sec, me = lax.axis_index("section"), lax.axis_index("ep")
    width, n_tok = tokens.shape
    n_sec = held.shape[1]
    feats, units = w_gate.shape
    z, y = me // 2, me % 2
    h = z // 2
    zz = z + h * (3 - 2 * z)
    x_peer = (sec + 2) % 4
    core_peer = sec + 1 - 2 * (sec % 2)
    y_peer = me + 1 - 2 * y
    inward = me + 2 - 4 * h
    outward = me - 2 + 4 * h
    split = n_tok // 2

    loads = [
        pltpu.make_async_copy(src, dst, w_sem.at[i])
        for i, (src, dst) in enumerate(((w_gate, wg), (w_up, wu), (w_down, wd)))
    ]
    for load in loads:
        load.start()

    barrier = pltpu.get_barrier_semaphore()

    def greet(**where):
        pl.semaphore_signal(barrier, inc=1, device_id=where, device_id_type=MESH)

    greet(section=x_peer)
    greet(section=core_peer)
    greet(ep=y_peer)
    greet(ep=inward)

    @pl.when(zz == 1)
    def _():
        greet(ep=outward)

    own = held.at[me, sec]
    own[:width, :] = tokens[...]
    own[width : 2 * width, :] = grad_out[...]
    n_ep = held.shape[0]
    expert = lax.broadcasted_iota(jnp.int32, (n_ep, n_tok), 0)
    weight = jnp.zeros((n_ep, n_tok), jnp.float32)
    for k in range(ids.shape[0]):
        weight = weight + jnp.where(ids[k : k + 1, :] == expert, probs[k : k + 1, :], 0.0)
    high = weight.astype(jnp.bfloat16).astype(jnp.float32)
    own[2 * width :, :] = jnp.concatenate([high, weight - high], axis=0).astype(jnp.bfloat16)

    @pl.when(zz == 0)
    def _():
        pl.semaphore_wait(barrier, 4)

    @pl.when(zz == 1)
    def _():
        pl.semaphore_wait(barrier, 5)

    def send(block, send_sem, recv_sem, **where):
        return pltpu.make_async_remote_copy(
            src_ref=block, dst_ref=block, send_sem=send_sem, recv_sem=recv_sem,
            device_id=where, device_id_type=MESH,
        )

    def source(k):
        s = k + (1 - k // 2) * ((k + zz) % 2 - k % 2)
        return s + h * (3 - 2 * s)

    def mine(k):
        return 2 * source(k) + y

    def other(k):
        return 2 * source(k) + 1 - y

    def upper(block):
        return block.at[:, pl.ds(0, split)]

    def lower(block):
        return block.at[:, pl.ds(split, split)]

    def z_in(k, idx):
        return send(held.at[mine(k), sec], z_send.at[0, idx], z_recv.at[idx], ep=inward)

    def z_out(k, idx):
        return send(held.at[mine(k), sec], z_send.at[1, idx], z_recv.at[idx], ep=outward)

    def x_whole(k):
        return send(held.at[mine(k), sec], x_send.at[k], x_recv.at[k], section=x_peer)

    def y_whole(k):
        return send(held.at[mine(k), sec], y_send.at[k], y_recv.at[k], ep=y_peer)

    def x_half(k):
        return send(upper(held.at[other(k), sec]), dx_send.at[k], dx_recv.at[k], section=x_peer)

    def y_half(k):
        return send(lower(held.at[mine(k), x_peer]), dy_send.at[k], dy_recv.at[k], ep=y_peer)

    def core(k, which):
        block = held.at[mine(k) if which < 2 else other(k), sec if which % 2 == 0 else x_peer]
        return send(block, c_send.at[k, which], c_recv.at[k, which], section=core_peer)

    def x_arrived(k):
        send(held.at[mine(k), x_peer], x_send.at[k], x_recv.at[k], section=x_peer).wait_recv()

    def y_arrived(k):
        send(held.at[other(k), sec], y_send.at[k], y_recv.at[k], ep=y_peer).wait_recv()

    def diagonal_arrived(k):
        block = held.at[other(k), x_peer]
        send(upper(block), dx_send.at[k], dx_recv.at[k], section=x_peer).wait_recv()
        send(lower(block), dy_send.at[k], dy_recv.at[k], ep=y_peer).wait_recv()

    def core_arrived(k, which):
        block = held.at[
            mine(k) if which < 2 else other(k),
            core_peer if which % 2 == 0 else (core_peer + 2) % 4,
        ]
        send(block, c_send.at[k, which], c_recv.at[k, which], section=core_peer).wait_recv()

    def column(k):
        x_whole(k).start()
        y_whole(k).start()
        core(k, 0).start()

    def forward(slot, at):
        here = pl.ds(at, n_tok)
        block = held.at[slot]
        parts = block[0, 2 * width :, :].astype(jnp.float32)
        which = lax.broadcasted_iota(jnp.int32, parts.shape, 0) % n_ep
        weight = jnp.sum(jnp.where(which == me, parts, 0.0), axis=0, keepdims=True)
        for s in range(n_sec):
            part = pl.ds(s * width, width)
            cols_in[part, here] = block[s, :width, :]
            cot = block[s, width : 2 * width, :].astype(jnp.float32)
            cols_scaled[part, here] = (weight * cot).astype(jnp.bfloat16)
        gate = jnp.dot(wg_t[...], cols_in[:, here], preferred_element_type=jnp.float32)
        linear = jnp.dot(wu_t[...], cols_in[:, here], preferred_element_type=jnp.float32)
        grad = jnp.dot(wd[...], cols_scaled[:, here], preferred_element_type=jnp.float32)
        sigma = jax.nn.sigmoid(gate)
        silu = gate * sigma
        term_hidden[:, here] = (silu * linear).astype(jnp.bfloat16)
        term_gate[:, here] = (grad * linear * sigma * (1.0 + gate * (1.0 - sigma))).astype(jnp.bfloat16)
        term_linear[:, here] = (grad * silu).astype(jnp.bfloat16)

    def outer(lhs, rhs):
        return lax.dot_general(lhs, rhs, (((1,), (1,)), ((), ())), preferred_element_type=jnp.float32)

    def weights():
        for at in range(0, units, TILE):
            to = min(units, at + TILE)
            acc_gate[:, at:to] += outer(cols_in[...], term_gate[at:to, :])
            acc_up[:, at:to] += outer(cols_in[...], term_linear[at:to, :])
        for at in range(0, feats, TILE):
            to = min(feats, at + TILE)
            acc_down[:, at:to] += outer(term_hidden[...], cols_scaled[at:to, :])

    z_in(0, 1 + zz).start()

    @pl.when(zz == 1)
    def _():
        z_out(0, 1).start()

    column(0)

    def clear(m, carry):
        part = feats // 6
        here = pl.ds(pl.multiple_of(m * part, 16), part)
        acc_gate[here, :] = jnp.zeros((part, units), jnp.float32)
        acc_up[here, :] = jnp.zeros((part, units), jnp.float32)
        return carry

    lax.fori_loop(0, 6, clear, 0)

    def clear_down(m, carry):
        part = units // 3
        here = pl.ds(pl.multiple_of(m * part, 16), part)
        acc_down[here, :] = jnp.zeros((part, feats), jnp.float32)
        return carry

    lax.fori_loop(0, 3, clear_down, 0)

    for load in loads:
        load.wait()
    for at in range(0, feats, TILE):
        to = min(feats, at + TILE)
        wg_t[:, at:to] = wg[at:to, :].T
        wu_t[:, at:to] = wu[at:to, :].T

    def step(k, carry):
        x_arrived(k)
        y_half(k).start()
        core(k, 1).start()
        y_arrived(k)
        x_half(k).start()
        core(k, 2).start()

        @pl.when(k < 3)
        def _():
            nxt = k + 1
            send(held.at[mine(nxt), sec], z_send.at[0, nxt], z_recv.at[nxt], ep=inward).wait_recv()

            @pl.when((zz == 1) & (nxt == 1))
            def _():
                z_in(nxt, 3).start()

            @pl.when((zz == 1) & (nxt >= 2))
            def _():
                z_out(nxt, nxt).start()

            column(nxt)

        core_arrived(k, 0)
        core_arrived(k, 1)
        forward(mine(k), 0)
        diagonal_arrived(k)
        core(k, 3).start()
        core_arrived(k, 2)
        core_arrived(k, 3)
        forward(other(k), n_tok)
        weights()
        return carry

    lax.fori_loop(0, 4, step, 0)

    def finish(m, carry):
        part = feats // 6
        here = pl.ds(pl.multiple_of(m * part, 16), part)
        out_gate[here, :] = acc_gate[here, :].astype(jnp.bfloat16)
        out_up[here, :] = acc_up[here, :].astype(jnp.bfloat16)
        return carry

    lax.fori_loop(0, 6, finish, 0)

    def finish_down(m, carry):
        part = units // 3
        here = pl.ds(pl.multiple_of(m * part, 16), part)
        out_down[here, :] = acc_down[here, :].astype(jnp.bfloat16)
        return carry

    lax.fori_loop(0, 3, finish_down, 0)

    z_in(0, 1 + zz).wait_send()

    @pl.when(zz == 1)
    def _():
        z_out(0, 1).wait_send()
        z_in(1, 3).wait_send()
        z_out(2, 2).wait_send()
        z_out(3, 3).wait_send()

    def drain(k, carry):
        x_whole(k).wait_send()
        y_whole(k).wait_send()
        x_half(k).wait_send()
        y_half(k).wait_send()
        for which in range(4):
            core(k, which).wait_send()
        return carry

    lax.fori_loop(0, 4, drain, 0)


def copy_kernel(*refs):
    srcs, dsts, sem = refs[:3], refs[3:6], refs[6]
    copies = [pltpu.make_async_copy(src, dst, sem.at[i]) for i, (src, dst) in enumerate(zip(srcs, dsts))]
    for copy in copies:
        copy.start()
    for copy in copies:
        copy.wait()


def fused(tokens, grad_out, expert_ids, probs, w_gate, w_up, w_down):
    n_ep, n_sec = lax.axis_size("ep"), lax.axis_size("section")
    n_tok, width = tokens.shape
    feats, units = w_gate.shape[1:]
    bf16, f32 = jnp.bfloat16, jnp.float32
    dma = pltpu.SemaphoreType.DMA
    vmem, hbm = pl.BlockSpec(memory_space=pltpu.VMEM), pl.BlockSpec(memory_space=pl.ANY)
    rows = n_ep * n_tok
    shapes = (
        jax.ShapeDtypeStruct((feats, units), bf16),
        jax.ShapeDtypeStruct((feats, units), bf16),
        jax.ShapeDtypeStruct((units, feats), bf16),
    )
    outs = pl.pallas_call(
        fused_kernel,
        out_shape=shapes,
        in_specs=[vmem] * 4 + [hbm] * 3,
        out_specs=(vmem,) * 3,
        scratch_shapes=[
            pltpu.VMEM((n_ep, n_sec, 2 * width + 2 * n_ep, n_tok), bf16),
            pltpu.VMEM((feats, units), bf16),
            pltpu.VMEM((feats, units), bf16),
            pltpu.VMEM((units, feats), bf16),
            pltpu.VMEM((units, feats), bf16),
            pltpu.VMEM((units, feats), bf16),
            pltpu.VMEM((feats, units), f32),
            pltpu.VMEM((feats, units), f32),
            pltpu.VMEM((units, feats), f32),
            pltpu.VMEM((feats, 2 * n_tok), bf16),
            pltpu.VMEM((feats, 2 * n_tok), bf16),
            pltpu.VMEM((units, 2 * n_tok), bf16),
            pltpu.VMEM((units, 2 * n_tok), bf16),
            pltpu.VMEM((units, 2 * n_tok), bf16),
            dma((3,)),
            dma((2, 4)), dma((4,)),
            dma((4,)), dma((4,)), dma((4,)), dma((4,)),
            dma((4,)), dma((4,)), dma((4,)), dma((4,)),
            dma((4, 4)), dma((4, 4)),
        ],
        cost_estimate=pl.CostEstimate(
            flops=12 * rows * feats * units, bytes_accessed=12 * feats * units, transcendentals=rows * units
        ),
        compiler_params=pltpu.CompilerParams(
            collective_id=0, has_side_effects=True, vmem_limit_bytes=60 * 1024 * 1024
        ),
    )(tokens.T, grad_out.T, expert_ids.T, probs.T, w_gate[0], w_up[0], w_down[0])
    outs = pl.pallas_call(
        copy_kernel,
        out_shape=shapes,
        in_specs=[hbm] * 3,
        out_specs=(hbm,) * 3,
        scratch_shapes=[dma((3,))],
        cost_estimate=pl.CostEstimate(flops=0, bytes_accessed=12 * feats * units, transcendentals=0),
        compiler_params=pltpu.CompilerParams(vmem_limit_bytes=60 * 1024 * 1024),
    )(*outs)
    return tuple(out[None] for out in outs)


def solution(mesh):
    body = shards
    if mesh.shape["ep"] == 8 and mesh.shape["section"] == 4:
        body = fused
    placed = (
        P("ep", "section"),
        P("ep", "section"),
        P("ep", None),
        P("ep", None),
        P("ep", None, "section"),
        P("ep", None, "section"),
        P("ep", "section", None),
    )
    return jax.shard_map(
        body,
        mesh=mesh,
        in_specs=placed,
        out_specs=(P("ep", None, "section"), P("ep", None, "section"), P("ep", "section", None)),
        check_vma=False,
    )
```

```python
import jax
import jax.numpy as jnp
from jax import lax
from jax.experimental import pallas as pl
from jax.experimental.pallas import tpu as pltpu
from jax.sharding import PartitionSpec as P


def rounded(value):
    return lax.optimization_barrier(value.astype(jnp.bfloat16)).astype(jnp.float32)


def slot_grads(inputs, scaled, gate_w, up_w, down_w):
    gate = jnp.einsum("hpscd,sdf->hpscf", inputs, gate_w, preferred_element_type=jnp.float32)
    linear = jnp.einsum("hpscd,sdf->hpscf", inputs, up_w, preferred_element_type=jnp.float32)
    sigma = jax.nn.sigmoid(gate)
    hidden = (gate * sigma * linear).astype(jnp.bfloat16)
    grad_hidden = jnp.einsum("hpscd,sfd->hpscf", scaled, down_w, preferred_element_type=jnp.float32)
    gate_term = (grad_hidden * linear * sigma * (1.0 + gate * (1.0 - sigma))).astype(jnp.bfloat16)
    linear_term = (grad_hidden * gate * sigma).astype(jnp.bfloat16)
    part_gate = rounded(
        jnp.einsum("hpscd,hpscf->hsdf", inputs, gate_term, preferred_element_type=jnp.float32)
    )
    part_up = rounded(
        jnp.einsum("hpscd,hpscf->hsdf", inputs, linear_term, preferred_element_type=jnp.float32)
    )
    part_down = rounded(
        jnp.einsum("hpscf,hpscd->hsfd", hidden, scaled, preferred_element_type=jnp.float32)
    )
    return (part_gate, part_up, part_down)


def shards(tokens, grad_out, expert_ids, probs, w_gate, w_up, w_down):
    n_ep = lax.axis_size("ep")
    half = n_ep // 2
    tok_dev, top = expert_ids.shape
    picks = tok_dev * top
    capacity = max(2, (3 * picks + 2 * n_ep - 1) // (2 * n_ep))
    flat_ids = expert_ids.reshape(picks)
    owners = jnp.arange(n_ep, dtype=jnp.int32)
    slots = 1
    matches = (flat_ids[:, None] == owners[None, :]).astype(jnp.int32)
    rank = jnp.sum(jnp.cumsum(matches, axis=0) * matches, axis=1) - 1
    position = flat_ids * slots * capacity + rank
    width = tokens.shape[1]
    rows = jnp.repeat(tokens, top, axis=0)
    scaled = (
        probs.reshape(picks, 1) * jnp.repeat(grad_out, top, axis=0).astype(jnp.float32)
    ).astype(jnp.bfloat16)
    buffer_rows = n_ep * slots * capacity
    send_rows = jnp.zeros((buffer_rows, width), jnp.bfloat16).at[position].set(rows)
    send_scaled = jnp.zeros((buffer_rows, width), jnp.bfloat16).at[position].set(scaled)
    send_rows = send_rows.reshape(n_ep, slots * capacity, width)
    send_scaled = send_scaled.reshape(n_ep, slots * capacity, width)
    got_rows, got_scaled = (
        lax.all_to_all(send_rows, "ep", split_axis=0, concat_axis=0, tiled=True),
        lax.all_to_all(send_scaled, "ep", split_axis=0, concat_axis=0, tiled=True),
    )
    got_rows = got_rows.reshape(2, half, slots, capacity, width)
    got_scaled = got_scaled.reshape(2, half, slots, capacity, width)
    inputs, scaled_rows = (
        lax.all_gather(got_rows, "section", axis=4, tiled=True),
        lax.all_gather(got_scaled, "section", axis=4, tiled=True),
    )
    part_gate, part_up, part_down = slot_grads(inputs, scaled_rows, w_gate, w_up, w_down)
    grad_gate = (part_gate[0] + part_gate[1]).astype(jnp.bfloat16)
    grad_up = (part_up[0] + part_up[1]).astype(jnp.bfloat16)
    grad_down = (part_down[0] + part_down[1]).astype(jnp.bfloat16)
    return (grad_gate, grad_up, grad_down)


MESH = pl.DeviceIdType.MESH
TILE = 256


def fused_kernel(
    tokens, grad_out, ids, probs, w_gate, w_up, w_down,
    out_gate, out_up, out_down,
    held, wg, wu, wd, wg_t, wu_t, acc_gate, acc_up, acc_down, cols_in, cols_scaled, term_gate, term_linear, term_hidden,
    w_sem, z_send, z_recv, x_send, x_recv, y_send, y_recv, dx_send, dx_recv, dy_send, dy_recv, c_send, c_recv, d_send, d_recv,
):
    sec, me = lax.axis_index("section"), lax.axis_index("ep")
    width, n_tok = tokens.shape
    n_sec = held.shape[1]
    feats, units = w_gate.shape
    z, y = me // 2, me % 2
    h = z // 2
    zz = z + h * (3 - 2 * z)
    x_peer = (sec + 2) % 4
    core_peer = sec + 1 - 2 * (sec % 2)
    y_peer = me + 1 - 2 * y
    inward = me + 2 - 4 * h
    outward = me - 2 + 4 * h
    block_rows = held.shape[2]
    half = block_rows // 2
    side = block_rows // 5 // 16 * 16
    along = block_rows - 2 * side

    loads = [
        pltpu.make_async_copy(src, dst, w_sem.at[i])
        for i, (src, dst) in enumerate(((w_gate, wg), (w_up, wu), (w_down, wd)))
    ]
    for load in loads:
        load.start()

    barrier = pltpu.get_barrier_semaphore()

    def greet(**where):
        pl.semaphore_signal(barrier, inc=1, device_id=where, device_id_type=MESH)

    greet(section=x_peer)
    greet(section=core_peer)
    greet(ep=y_peer)
    greet(ep=inward)

    @pl.when(zz == 1)
    def _():
        greet(ep=outward)

    own = held.at[me, sec]
    own[:width, :] = tokens[...]
    own[width : 2 * width, :] = grad_out[...]
    n_ep = held.shape[0]
    expert = lax.broadcasted_iota(jnp.int32, (n_ep, n_tok), 0)
    weight = jnp.zeros((n_ep, n_tok), jnp.float32)
    for k in range(ids.shape[0]):
        weight = weight + jnp.where(ids[k : k + 1, :] == expert, probs[k : k + 1, :], 0.0)
    high = weight.astype(jnp.bfloat16).astype(jnp.float32)
    own[2 * width :, :] = jnp.concatenate([high, weight - high], axis=0).astype(jnp.bfloat16)

    @pl.when(zz == 0)
    def _():
        pl.semaphore_wait(barrier, 4)

    @pl.when(zz == 1)
    def _():
        pl.semaphore_wait(barrier, 5)

    def send(block, send_sem, recv_sem, **where):
        return pltpu.make_async_remote_copy(
            src_ref=block, dst_ref=block, send_sem=send_sem, recv_sem=recv_sem,
            device_id=where, device_id_type=MESH,
        )

    def source(k):
        s = k + (1 - k // 2) * ((k + zz) % 2 - k % 2)
        return s + h * (3 - 2 * s)

    def mine(k):
        return 2 * source(k) + y

    def other(k):
        return 2 * source(k) + 1 - y

    def upper(block, first):
        return block.at[pl.ds(0, half)] if first else block.at[pl.ds(along, side)]

    def lower(block, first):
        return block.at[pl.ds(half, half)] if first else block.at[pl.ds(along + side, side)]

    def d_block(k):
        return held.at[other(k), x_peer, pl.ds(0, along)]

    def d_in(k, idx):
        return send(d_block(k), d_send.at[0, idx], d_recv.at[idx], ep=inward)

    def d_out(k, idx):
        return send(d_block(k), d_send.at[1, idx], d_recv.at[idx], ep=outward)

    def d_arrived(k):
        send(d_block(k), d_send.at[0, k], d_recv.at[k], ep=inward).wait_recv()

    def z_arrived(k):
        send(held.at[mine(k), sec], z_send.at[0, k], z_recv.at[k], ep=inward).wait_recv()

    def z_in(k, idx):
        return send(held.at[mine(k), sec], z_send.at[0, idx], z_recv.at[idx], ep=inward)

    def z_out(k, idx):
        return send(held.at[mine(k), sec], z_send.at[1, idx], z_recv.at[idx], ep=outward)

    def x_whole(k):
        return send(held.at[mine(k), sec], x_send.at[k], x_recv.at[k], section=x_peer)

    def y_whole(k):
        return send(held.at[mine(k), sec], y_send.at[k], y_recv.at[k], ep=y_peer)

    def x_half(k, first):
        return send(upper(held.at[other(k), sec], first), dx_send.at[k], dx_recv.at[k], section=x_peer)

    def y_half(k, first):
        return send(lower(held.at[mine(k), x_peer], first), dy_send.at[k], dy_recv.at[k], ep=y_peer)

    def by_step(k, act):
        @pl.when(k == 0)
        def _():
            act(True)

        @pl.when(k > 0)
        def _():
            act(False)

    def core(k, which):
        block = held.at[mine(k) if which < 2 else other(k), sec if which % 2 == 0 else x_peer]
        return send(block, c_send.at[k, which], c_recv.at[k, which], section=core_peer)

    def x_arrived(k):
        send(held.at[mine(k), x_peer], x_send.at[k], x_recv.at[k], section=x_peer).wait_recv()

    def y_arrived(k):
        send(held.at[other(k), sec], y_send.at[k], y_recv.at[k], ep=y_peer).wait_recv()

    def diagonal_arrived(k):
        block = held.at[other(k), x_peer]

        def sides(first):
            send(upper(block, first), dx_send.at[k], dx_recv.at[k], section=x_peer).wait_recv()
            send(lower(block, first), dy_send.at[k], dy_recv.at[k], ep=y_peer).wait_recv()

        by_step(k, sides)

        @pl.when((zz == 0) & (k > 0))
        def _():
            d_arrived(k)

    def core_arrived(k, which):
        block = held.at[
            mine(k) if which < 2 else other(k),
            core_peer if which % 2 == 0 else (core_peer + 2) % 4,
        ]
        send(block, c_send.at[k, which], c_recv.at[k, which], section=core_peer).wait_recv()

    def column(k):
        x_whole(k).start()
        y_whole(k).start()
        core(k, 0).start()

    def forward(slot, at):
        here = pl.ds(at, n_tok)
        block = held.at[slot]
        parts = block[0, 2 * width :, :].astype(jnp.float32)
        which = lax.broadcasted_iota(jnp.int32, parts.shape, 0) % n_ep
        weight = jnp.sum(jnp.where(which == me, parts, 0.0), axis=0, keepdims=True)
        for s in range(n_sec):
            part = pl.ds(s * width, width)
            cols_in[part, here] = block[s, :width, :]
            cot = block[s, width : 2 * width, :].astype(jnp.float32)
            cols_scaled[part, here] = (weight * cot).astype(jnp.bfloat16)
        gate = jnp.dot(wg_t[...], cols_in[:, here], preferred_element_type=jnp.float32)
        linear = jnp.dot(wu_t[...], cols_in[:, here], preferred_element_type=jnp.float32)
        grad = jnp.dot(wd[...], cols_scaled[:, here], preferred_element_type=jnp.float32)
        sigma = jax.nn.sigmoid(gate)
        silu = gate * sigma
        term_hidden[:, here] = (silu * linear).astype(jnp.bfloat16)
        term_gate[:, here] = (grad * linear * sigma * (1.0 + gate * (1.0 - sigma))).astype(jnp.bfloat16)
        term_linear[:, here] = (grad * silu).astype(jnp.bfloat16)

    def outer(lhs, rhs):
        return lax.dot_general(lhs, rhs, (((1,), (1,)), ((), ())), preferred_element_type=jnp.float32)

    def weights():
        for at in range(0, units, TILE):
            to = min(units, at + TILE)
            acc_gate[:, at:to] += outer(cols_in[...], term_gate[at:to, :])
            acc_up[:, at:to] += outer(cols_in[...], term_linear[at:to, :])
        for at in range(0, feats, TILE):
            to = min(feats, at + TILE)
            acc_down[:, at:to] += outer(term_hidden[...], cols_scaled[at:to, :])

    z_in(0, 1 + zz).start()

    @pl.when(zz == 1)
    def _():
        z_out(0, 1).start()

    column(0)

    def clear(m, carry):
        part = feats // 6
        here = pl.ds(pl.multiple_of(m * part, 16), part)
        acc_gate[here, :] = jnp.zeros((part, units), jnp.float32)
        acc_up[here, :] = jnp.zeros((part, units), jnp.float32)
        return carry

    lax.fori_loop(0, 6, clear, 0)

    def clear_down(m, carry):
        part = units // 3
        here = pl.ds(pl.multiple_of(m * part, 16), part)
        acc_down[here, :] = jnp.zeros((part, feats), jnp.float32)
        return carry

    lax.fori_loop(0, 3, clear_down, 0)

    for load in loads:
        load.wait()
    for at in range(0, feats, TILE):
        to = min(feats, at + TILE)
        wg_t[:, at:to] = wg[at:to, :].T
        wu_t[:, at:to] = wu[at:to, :].T

    def step(k, carry):
        x_arrived(k)
        by_step(k, lambda first: y_half(k, first).start())
        core(k, 1).start()
        y_arrived(k)
        by_step(k, lambda first: x_half(k, first).start())
        core(k, 2).start()

        @pl.when(k < 3)
        def _():
            nxt = k + 1

            @pl.when((zz == 0) | (nxt == 1))
            def _():
                z_arrived(nxt)

            @pl.when((zz == 1) & (nxt == 1))
            def _():
                z_in(1, 3).start()
                z_arrived(2)
                z_out(2, 2).start()

            column(nxt)

        @pl.when((zz == 1) & (k == 1))
        def _():
            d_arrived(1)
            d_in(1, 3).start()
            d_arrived(2)
            d_out(2, 2).start()

        core_arrived(k, 0)
        core_arrived(k, 1)
        forward(mine(k), 0)
        diagonal_arrived(k)
        core(k, 3).start()

        @pl.when(k == 0)
        def _():
            d_in(0, 1 + zz).start()

            @pl.when(zz == 1)
            def _():
                d_out(0, 1).start()
                z_arrived(3)
                z_out(3, 3).start()

        core_arrived(k, 2)
        core_arrived(k, 3)
        forward(other(k), n_tok)

        @pl.when((zz == 1) & (k == 1))
        def _():
            d_arrived(3)
            d_out(3, 3).start()

        weights()
        return carry

    lax.fori_loop(0, 4, step, 0)

    def finish(m, carry):
        part = feats // 6
        here = pl.ds(pl.multiple_of(m * part, 16), part)
        out_gate[here, :] = acc_gate[here, :].astype(jnp.bfloat16)
        out_up[here, :] = acc_up[here, :].astype(jnp.bfloat16)
        return carry

    lax.fori_loop(0, 6, finish, 0)

    def finish_down(m, carry):
        part = units // 3
        here = pl.ds(pl.multiple_of(m * part, 16), part)
        out_down[here, :] = acc_down[here, :].astype(jnp.bfloat16)
        return carry

    lax.fori_loop(0, 3, finish_down, 0)

    z_in(0, 1 + zz).wait_send()
    d_in(0, 1 + zz).wait_send()

    @pl.when(zz == 1)
    def _():
        z_out(0, 1).wait_send()
        z_in(1, 3).wait_send()
        z_out(2, 2).wait_send()
        z_out(3, 3).wait_send()
        d_out(0, 1).wait_send()
        d_in(1, 3).wait_send()
        d_out(2, 2).wait_send()
        d_out(3, 3).wait_send()

    def drain(k, carry):
        x_whole(k).wait_send()
        y_whole(k).wait_send()

        def sides(first):
            x_half(k, first).wait_send()
            y_half(k, first).wait_send()

        by_step(k, sides)
        for which in range(4):
            core(k, which).wait_send()
        return carry

    lax.fori_loop(0, 4, drain, 0)


def copy_kernel(gate, up, down, out_gate, out_up, out_down):
    out_gate[...] = gate[...]
    out_up[...] = up[...]
    out_down[...] = down[...]


def fused(tokens, grad_out, expert_ids, probs, w_gate, w_up, w_down):
    n_ep, n_sec = lax.axis_size("ep"), lax.axis_size("section")
    n_tok, width = tokens.shape
    feats, units = w_gate.shape[1:]
    bf16, f32 = jnp.bfloat16, jnp.float32
    dma = pltpu.SemaphoreType.DMA
    vmem, hbm = pl.BlockSpec(memory_space=pltpu.VMEM), pl.BlockSpec(memory_space=pl.ANY)
    rows = n_ep * n_tok
    shapes = (
        jax.ShapeDtypeStruct((feats, units), bf16),
        jax.ShapeDtypeStruct((feats, units), bf16),
        jax.ShapeDtypeStruct((units, feats), bf16),
    )
    outs = pl.pallas_call(
        fused_kernel,
        out_shape=shapes,
        in_specs=[vmem] * 4 + [hbm] * 3,
        out_specs=(vmem,) * 3,
        scratch_shapes=[
            pltpu.VMEM((n_ep, n_sec, 2 * width + 2 * n_ep, n_tok), bf16),
            pltpu.VMEM((feats, units), bf16),
            pltpu.VMEM((feats, units), bf16),
            pltpu.VMEM((units, feats), bf16),
            pltpu.VMEM((units, feats), bf16),
            pltpu.VMEM((units, feats), bf16),
            pltpu.VMEM((feats, units), f32),
            pltpu.VMEM((feats, units), f32),
            pltpu.VMEM((units, feats), f32),
            pltpu.VMEM((feats, 2 * n_tok), bf16),
            pltpu.VMEM((feats, 2 * n_tok), bf16),
            pltpu.VMEM((units, 2 * n_tok), bf16),
            pltpu.VMEM((units, 2 * n_tok), bf16),
            pltpu.VMEM((units, 2 * n_tok), bf16),
            dma((3,)),
            dma((2, 4)), dma((4,)),
            dma((4,)), dma((4,)), dma((4,)), dma((4,)),
            dma((4,)), dma((4,)), dma((4,)), dma((4,)),
            dma((4, 4)), dma((4, 4)),
            dma((2, 4)), dma((4,)),
        ],
        cost_estimate=pl.CostEstimate(
            flops=12 * rows * feats * units, bytes_accessed=12 * feats * units, transcendentals=rows * units
        ),
        compiler_params=pltpu.CompilerParams(
            collective_id=0, has_side_effects=True, vmem_limit_bytes=60 * 1024 * 1024
        ),
    )(tokens.T, grad_out.T, expert_ids.T, probs.T, w_gate[0], w_up[0], w_down[0])
    blocks = [pl.BlockSpec((size // 5, other), lambda i: (i, 0)) for size, other in ((feats, units), (feats, units), (units, feats))]
    outs = pl.pallas_call(
        copy_kernel,
        out_shape=shapes,
        grid=(5,),
        in_specs=blocks,
        out_specs=tuple(blocks),
        cost_estimate=pl.CostEstimate(flops=0, bytes_accessed=12 * feats * units, transcendentals=0),
        compiler_params=pltpu.CompilerParams(vmem_limit_bytes=60 * 1024 * 1024),
    )(*outs)
    return tuple(out[None] for out in outs)


def solution(mesh):
    body = shards
    if mesh.shape["ep"] == 8 and mesh.shape["section"] == 4:
        body = fused
    placed = (
        P("ep", "section"),
        P("ep", "section"),
        P("ep", None),
        P("ep", None),
        P("ep", None, "section"),
        P("ep", None, "section"),
        P("ep", "section", None),
    )
    return jax.shard_map(
        body,
        mesh=mesh,
        in_specs=placed,
        out_specs=(P("ep", None, "section"), P("ep", None, "section"), P("ep", "section", None)),
        check_vma=False,
    )
```

```python
import jax
import jax.numpy as jnp
from jax import lax
from jax.experimental import pallas as pl
from jax.experimental.pallas import tpu as pltpu
from jax.sharding import PartitionSpec as P


def rounded(value):
    return lax.optimization_barrier(value.astype(jnp.bfloat16)).astype(jnp.float32)


def slot_grads(inputs, scaled, gate_w, up_w, down_w):
    gate = jnp.einsum("hpscd,sdf->hpscf", inputs, gate_w, preferred_element_type=jnp.float32)
    linear = jnp.einsum("hpscd,sdf->hpscf", inputs, up_w, preferred_element_type=jnp.float32)
    sigma = jax.nn.sigmoid(gate)
    hidden = (gate * sigma * linear).astype(jnp.bfloat16)
    grad_hidden = jnp.einsum("hpscd,sfd->hpscf", scaled, down_w, preferred_element_type=jnp.float32)
    gate_term = (grad_hidden * linear * sigma * (1.0 + gate * (1.0 - sigma))).astype(jnp.bfloat16)
    linear_term = (grad_hidden * gate * sigma).astype(jnp.bfloat16)
    part_gate = rounded(
        jnp.einsum("hpscd,hpscf->hsdf", inputs, gate_term, preferred_element_type=jnp.float32)
    )
    part_up = rounded(
        jnp.einsum("hpscd,hpscf->hsdf", inputs, linear_term, preferred_element_type=jnp.float32)
    )
    part_down = rounded(
        jnp.einsum("hpscf,hpscd->hsfd", hidden, scaled, preferred_element_type=jnp.float32)
    )
    return (part_gate, part_up, part_down)


def shards(tokens, grad_out, expert_ids, probs, w_gate, w_up, w_down):
    n_ep = lax.axis_size("ep")
    half = n_ep // 2
    tok_dev, top = expert_ids.shape
    picks = tok_dev * top
    capacity = max(2, (3 * picks + 2 * n_ep - 1) // (2 * n_ep))
    flat_ids = expert_ids.reshape(picks)
    owners = jnp.arange(n_ep, dtype=jnp.int32)
    slots = 1
    matches = (flat_ids[:, None] == owners[None, :]).astype(jnp.int32)
    rank = jnp.sum(jnp.cumsum(matches, axis=0) * matches, axis=1) - 1
    position = flat_ids * slots * capacity + rank
    width = tokens.shape[1]
    rows = jnp.repeat(tokens, top, axis=0)
    scaled = (
        probs.reshape(picks, 1) * jnp.repeat(grad_out, top, axis=0).astype(jnp.float32)
    ).astype(jnp.bfloat16)
    buffer_rows = n_ep * slots * capacity
    send_rows = jnp.zeros((buffer_rows, width), jnp.bfloat16).at[position].set(rows)
    send_scaled = jnp.zeros((buffer_rows, width), jnp.bfloat16).at[position].set(scaled)
    send_rows = send_rows.reshape(n_ep, slots * capacity, width)
    send_scaled = send_scaled.reshape(n_ep, slots * capacity, width)
    got_rows, got_scaled = (
        lax.all_to_all(send_rows, "ep", split_axis=0, concat_axis=0, tiled=True),
        lax.all_to_all(send_scaled, "ep", split_axis=0, concat_axis=0, tiled=True),
    )
    got_rows = got_rows.reshape(2, half, slots, capacity, width)
    got_scaled = got_scaled.reshape(2, half, slots, capacity, width)
    inputs, scaled_rows = (
        lax.all_gather(got_rows, "section", axis=4, tiled=True),
        lax.all_gather(got_scaled, "section", axis=4, tiled=True),
    )
    part_gate, part_up, part_down = slot_grads(inputs, scaled_rows, w_gate, w_up, w_down)
    grad_gate = (part_gate[0] + part_gate[1]).astype(jnp.bfloat16)
    grad_up = (part_up[0] + part_up[1]).astype(jnp.bfloat16)
    grad_down = (part_down[0] + part_down[1]).astype(jnp.bfloat16)
    return (grad_gate, grad_up, grad_down)


MESH = pl.DeviceIdType.MESH
TILE = 256


def fused_kernel(
    tokens, grad_out, ids, probs, w_gate, w_up, w_down,
    out_gate, out_up, out_down, out_in, out_scaled, out_term_gate, out_term_linear, out_term_hidden,
    held, wg, wu, wd, wg_t, wu_t, acc_gate, acc_up, acc_down, cols_in, cols_scaled, term_gate, term_linear, term_hidden,
    part_gate, part_up, part_down, out_sem, w_sem, z_send, z_recv, x_send, x_recv, y_send, y_recv, dx_send, dx_recv, dy_send, dy_recv, c_send, c_recv, d_send, d_recv,
):
    sec, me = lax.axis_index("section"), lax.axis_index("ep")
    width, n_tok = tokens.shape
    n_sec = held.shape[1]
    feats, units = w_gate.shape
    z, y = me // 2, me % 2
    h = z // 2
    zz = z + h * (3 - 2 * z)
    x_peer = (sec + 2) % 4
    core_peer = sec + 1 - 2 * (sec % 2)
    y_peer = me + 1 - 2 * y
    inward = me + 2 - 4 * h
    outward = me - 2 + 4 * h
    block_rows = held.shape[2]
    half = block_rows // 2
    side = block_rows // 5 // 16 * 16
    along = block_rows - 2 * side

    loads = [
        pltpu.make_async_copy(src, dst, w_sem.at[i])
        for i, (src, dst) in enumerate(((w_gate, wg), (w_up, wu), (w_down, wd)))
    ]
    for load in loads:
        load.start()

    barrier = pltpu.get_barrier_semaphore()

    def greet(**where):
        pl.semaphore_signal(barrier, inc=1, device_id=where, device_id_type=MESH)

    greet(section=x_peer)
    greet(section=core_peer)
    greet(ep=y_peer)
    greet(ep=inward)

    @pl.when(zz == 1)
    def _():
        greet(ep=outward)

    own = held.at[me, sec]
    own[:width, :] = tokens[...]
    own[width : 2 * width, :] = grad_out[...]
    n_ep = held.shape[0]
    expert = lax.broadcasted_iota(jnp.int32, (n_ep, n_tok), 0)
    weight = jnp.zeros((n_ep, n_tok), jnp.float32)
    for k in range(ids.shape[0]):
        weight = weight + jnp.where(ids[k : k + 1, :] == expert, probs[k : k + 1, :], 0.0)
    high = weight.astype(jnp.bfloat16).astype(jnp.float32)
    own[2 * width :, :] = jnp.concatenate([high, weight - high], axis=0).astype(jnp.bfloat16)

    @pl.when(zz == 0)
    def _():
        pl.semaphore_wait(barrier, 4)

    @pl.when(zz == 1)
    def _():
        pl.semaphore_wait(barrier, 5)

    def send(block, send_sem, recv_sem, **where):
        return pltpu.make_async_remote_copy(
            src_ref=block, dst_ref=block, send_sem=send_sem, recv_sem=recv_sem,
            device_id=where, device_id_type=MESH,
        )

    def source(k):
        s = k + (1 - k // 2) * ((k + zz) % 2 - k % 2)
        return s + h * (3 - 2 * s)

    def mine(k):
        return 2 * source(k) + y

    def other(k):
        return 2 * source(k) + 1 - y

    def upper(block, first):
        return block.at[pl.ds(0, half)] if first else block.at[pl.ds(along, side)]

    def lower(block, first):
        return block.at[pl.ds(half, half)] if first else block.at[pl.ds(along + side, side)]

    def d_block(k):
        return held.at[other(k), x_peer, pl.ds(0, along)]

    def d_in(k, idx):
        return send(d_block(k), d_send.at[0, idx], d_recv.at[idx], ep=inward)

    def d_out(k, idx):
        return send(d_block(k), d_send.at[1, idx], d_recv.at[idx], ep=outward)

    def d_arrived(k):
        send(d_block(k), d_send.at[0, k], d_recv.at[k], ep=inward).wait_recv()

    def z_arrived(k):
        send(held.at[mine(k), sec], z_send.at[0, k], z_recv.at[k], ep=inward).wait_recv()

    def z_in(k, idx):
        return send(held.at[mine(k), sec], z_send.at[0, idx], z_recv.at[idx], ep=inward)

    def z_out(k, idx):
        return send(held.at[mine(k), sec], z_send.at[1, idx], z_recv.at[idx], ep=outward)

    def x_whole(k):
        return send(held.at[mine(k), sec], x_send.at[k], x_recv.at[k], section=x_peer)

    def y_whole(k):
        return send(held.at[mine(k), sec], y_send.at[k], y_recv.at[k], ep=y_peer)

    def x_half(k, first):
        return send(upper(held.at[other(k), sec], first), dx_send.at[k], dx_recv.at[k], section=x_peer)

    def y_half(k, first):
        return send(lower(held.at[mine(k), x_peer], first), dy_send.at[k], dy_recv.at[k], ep=y_peer)

    def by_step(k, act):
        @pl.when(k == 0)
        def _():
            act(True)

        @pl.when(k > 0)
        def _():
            act(False)

    def core(k, which):
        block = held.at[mine(k) if which < 2 else other(k), sec if which % 2 == 0 else x_peer]
        return send(block, c_send.at[k, which], c_recv.at[k, which], section=core_peer)

    def x_arrived(k):
        send(held.at[mine(k), x_peer], x_send.at[k], x_recv.at[k], section=x_peer).wait_recv()

    def y_arrived(k):
        send(held.at[other(k), sec], y_send.at[k], y_recv.at[k], ep=y_peer).wait_recv()

    def diagonal_arrived(k):
        block = held.at[other(k), x_peer]

        def sides(first):
            send(upper(block, first), dx_send.at[k], dx_recv.at[k], section=x_peer).wait_recv()
            send(lower(block, first), dy_send.at[k], dy_recv.at[k], ep=y_peer).wait_recv()

        by_step(k, sides)

        @pl.when((zz == 0) & (k > 0))
        def _():
            d_arrived(k)

    def core_arrived(k, which):
        block = held.at[
            mine(k) if which < 2 else other(k),
            core_peer if which % 2 == 0 else (core_peer + 2) % 4,
        ]
        send(block, c_send.at[k, which], c_recv.at[k, which], section=core_peer).wait_recv()

    def column(k):
        x_whole(k).start()
        y_whole(k).start()
        core(k, 0).start()

    def forward(slot, at):
        here = pl.ds(at, n_tok)
        block = held.at[slot]
        parts = block[0, 2 * width :, :].astype(jnp.float32)
        which = lax.broadcasted_iota(jnp.int32, parts.shape, 0) % n_ep
        weight = jnp.sum(jnp.where(which == me, parts, 0.0), axis=0, keepdims=True)
        for s in range(n_sec):
            part = pl.ds(s * width, width)
            cols_in[part, here] = block[s, :width, :]
            cot = block[s, width : 2 * width, :].astype(jnp.float32)
            cols_scaled[part, here] = (weight * cot).astype(jnp.bfloat16)
        gate = jnp.dot(wg_t[...], cols_in[:, here], preferred_element_type=jnp.float32)
        linear = jnp.dot(wu_t[...], cols_in[:, here], preferred_element_type=jnp.float32)
        grad = jnp.dot(wd[...], cols_scaled[:, here], preferred_element_type=jnp.float32)
        sigma = jax.nn.sigmoid(gate)
        silu = gate * sigma
        term_hidden[:, here] = (silu * linear).astype(jnp.bfloat16)
        term_gate[:, here] = (grad * linear * sigma * (1.0 + gate * (1.0 - sigma))).astype(jnp.bfloat16)
        term_linear[:, here] = (grad * silu).astype(jnp.bfloat16)

    def outer(lhs, rhs):
        return lax.dot_general(lhs, rhs, (((1,), (1,)), ((), ())), preferred_element_type=jnp.float32)

    def weights():
        for at in range(0, units, TILE):
            to = min(units, at + TILE)
            acc_gate[:, at:to] += outer(cols_in[...], term_gate[at:to, :])
            acc_up[:, at:to] += outer(cols_in[...], term_linear[at:to, :])
        for at in range(0, feats, TILE):
            to = min(feats, at + TILE)
            acc_down[:, at:to] += outer(term_hidden[...], cols_scaled[at:to, :])

    z_in(0, 1 + zz).start()

    @pl.when(zz == 1)
    def _():
        z_out(0, 1).start()

    column(0)

    def clear(m, carry):
        part = feats // 6
        here = pl.ds(pl.multiple_of(m * part, 16), part)
        acc_gate[here, :] = jnp.zeros((part, units), jnp.float32)
        acc_up[here, :] = jnp.zeros((part, units), jnp.float32)
        return carry

    lax.fori_loop(0, 6, clear, 0)

    def clear_down(m, carry):
        part = units // 3
        here = pl.ds(pl.multiple_of(m * part, 16), part)
        acc_down[here, :] = jnp.zeros((part, feats), jnp.float32)
        return carry

    lax.fori_loop(0, 3, clear_down, 0)

    for load in loads:
        load.wait()
    for at in range(0, feats, TILE):
        to = min(feats, at + TILE)
        wg_t[:, at:to] = wg[at:to, :].T
        wu_t[:, at:to] = wu[at:to, :].T

    def finish(m, carry):
        part = feats // 6
        here = pl.ds(pl.multiple_of(m * part, 16), part)
        part_gate[here, :] = acc_gate[here, :].astype(jnp.bfloat16)
        part_up[here, :] = acc_up[here, :].astype(jnp.bfloat16)
        return carry

    def finish_down(m, carry):
        part = units // 3
        here = pl.ds(pl.multiple_of(m * part, 16), part)
        part_down[here, :] = acc_down[here, :].astype(jnp.bfloat16)
        return carry

    pairs = (
        (part_gate, out_gate), (part_up, out_up), (part_down, out_down), (cols_in, out_in), (cols_scaled, out_scaled),
        (term_gate, out_term_gate), (term_linear, out_term_linear), (term_hidden, out_term_hidden),
    )
    results = [pltpu.make_async_copy(src, dst, out_sem.at[i]) for i, (src, dst) in enumerate(pairs)]

    def step(k, carry):
        x_arrived(k)
        by_step(k, lambda first: y_half(k, first).start())
        core(k, 1).start()
        y_arrived(k)
        by_step(k, lambda first: x_half(k, first).start())
        core(k, 2).start()

        @pl.when(k < 3)
        def _():
            nxt = k + 1

            @pl.when((zz == 0) | (nxt == 1))
            def _():
                z_arrived(nxt)

            @pl.when((zz == 1) & (nxt == 1))
            def _():
                z_in(1, 3).start()
                z_arrived(2)
                z_out(2, 2).start()

            column(nxt)

        @pl.when((zz == 1) & (k == 1))
        def _():
            d_arrived(1)
            d_in(1, 3).start()
            d_arrived(2)
            d_out(2, 2).start()

        core_arrived(k, 0)
        core_arrived(k, 1)
        forward(mine(k), 0)
        diagonal_arrived(k)
        core(k, 3).start()

        @pl.when(k == 0)
        def _():
            d_in(0, 1 + zz).start()

            @pl.when(zz == 1)
            def _():
                d_out(0, 1).start()
                z_arrived(3)
                z_out(3, 3).start()

        core_arrived(k, 2)
        core_arrived(k, 3)
        forward(other(k), n_tok)

        @pl.when((zz == 1) & (k == 1))
        def _():
            d_arrived(3)
            d_out(3, 3).start()

        @pl.when(k < 3)
        def _():
            weights()

        @pl.when(k == 2)
        def _():
            lax.fori_loop(0, 6, finish, 0)
            lax.fori_loop(0, 3, finish_down, 0)
            for result in results[:3]:
                result.start()

        return carry

    lax.fori_loop(0, 4, step, 0)

    for result in results[3:]:
        result.start()
    z_in(0, 1 + zz).wait_send()
    d_in(0, 1 + zz).wait_send()

    @pl.when(zz == 1)
    def _():
        z_out(0, 1).wait_send()
        z_in(1, 3).wait_send()
        z_out(2, 2).wait_send()
        z_out(3, 3).wait_send()
        d_out(0, 1).wait_send()
        d_in(1, 3).wait_send()
        d_out(2, 2).wait_send()
        d_out(3, 3).wait_send()

    def drain(k, carry):
        x_whole(k).wait_send()
        y_whole(k).wait_send()

        def sides(first):
            x_half(k, first).wait_send()
            y_half(k, first).wait_send()

        by_step(k, sides)
        for which in range(4):
            core(k, which).wait_send()
        return carry

    lax.fori_loop(0, 4, drain, 0)
    for result in results:
        result.wait()


def last_kernel(
    part_gate, part_up, part_down, cols_in, cols_scaled, term_gate, term_linear, term_hidden, out_gate, out_up, out_down
):
    def outer(lhs, rhs):
        return lax.dot_general(lhs, rhs, (((1,), (1,)), ((), ())), preferred_element_type=jnp.float32)

    for part, out, lhs, rhs in (
        (part_gate, out_gate, cols_in, term_gate),
        (part_up, out_up, cols_in, term_linear),
        (part_down, out_down, term_hidden, cols_scaled),
    ):
        out[...] = (part[...].astype(jnp.float32) + outer(lhs[...], rhs[...])).astype(jnp.bfloat16)


def fused(tokens, grad_out, expert_ids, probs, w_gate, w_up, w_down):
    n_ep, n_sec = lax.axis_size("ep"), lax.axis_size("section")
    n_tok, width = tokens.shape
    feats, units = w_gate.shape[1:]
    bf16, f32 = jnp.bfloat16, jnp.float32
    dma = pltpu.SemaphoreType.DMA
    vmem, hbm = pl.BlockSpec(memory_space=pltpu.VMEM), pl.BlockSpec(memory_space=pl.ANY)
    rows = n_ep * n_tok
    shapes = (
        jax.ShapeDtypeStruct((feats, units), bf16),
        jax.ShapeDtypeStruct((feats, units), bf16),
        jax.ShapeDtypeStruct((units, feats), bf16),
    )
    outs = pl.pallas_call(
        fused_kernel,
        out_shape=shapes
        + tuple(jax.ShapeDtypeStruct((size, 2 * n_tok), bf16) for size in (feats, feats, units, units, units)),
        in_specs=[vmem] * 4 + [hbm] * 3,
        out_specs=(hbm,) * 8,
        scratch_shapes=[
            pltpu.VMEM((n_ep, n_sec, 2 * width + 2 * n_ep, n_tok), bf16),
            pltpu.VMEM((feats, units), bf16),
            pltpu.VMEM((feats, units), bf16),
            pltpu.VMEM((units, feats), bf16),
            pltpu.VMEM((units, feats), bf16),
            pltpu.VMEM((units, feats), bf16),
            pltpu.VMEM((feats, units), f32),
            pltpu.VMEM((feats, units), f32),
            pltpu.VMEM((units, feats), f32),
            pltpu.VMEM((feats, 2 * n_tok), bf16),
            pltpu.VMEM((feats, 2 * n_tok), bf16),
            pltpu.VMEM((units, 2 * n_tok), bf16),
            pltpu.VMEM((units, 2 * n_tok), bf16),
            pltpu.VMEM((units, 2 * n_tok), bf16),
            pltpu.VMEM((feats, units), bf16),
            pltpu.VMEM((feats, units), bf16),
            pltpu.VMEM((units, feats), bf16),
            dma((8,)),
            dma((3,)),
            dma((2, 4)), dma((4,)),
            dma((4,)), dma((4,)), dma((4,)), dma((4,)),
            dma((4,)), dma((4,)), dma((4,)), dma((4,)),
            dma((4, 4)), dma((4, 4)),
            dma((2, 4)), dma((4,)),
        ],
        cost_estimate=pl.CostEstimate(
            flops=12 * rows * feats * units, bytes_accessed=12 * feats * units, transcendentals=rows * units
        ),
        compiler_params=pltpu.CompilerParams(
            collective_id=0, has_side_effects=True, vmem_limit_bytes=60 * 1024 * 1024
        ),
    )(tokens.T, grad_out.T, expert_ids.T, probs.T, w_gate[0], w_up[0], w_down[0])
    steps = 5

    def by_rows(size, other):
        return pl.BlockSpec((size // steps, other), lambda i: (i, 0))

    def whole(size):
        return pl.BlockSpec((size, 2 * n_tok), lambda i: (0, 0))

    blocks = [by_rows(feats, units), by_rows(feats, units), by_rows(units, feats)]
    outs = pl.pallas_call(
        last_kernel,
        out_shape=shapes,
        grid=(steps,),
        in_specs=blocks
        + [by_rows(feats, 2 * n_tok), whole(feats), whole(units), whole(units), by_rows(units, 2 * n_tok)],
        out_specs=tuple(blocks),
        cost_estimate=pl.CostEstimate(
            flops=12 * n_tok * feats * units, bytes_accessed=12 * feats * units, transcendentals=0
        ),
        compiler_params=pltpu.CompilerParams(vmem_limit_bytes=60 * 1024 * 1024),
    )(*outs)
    return tuple(out[None] for out in outs)


def solution(mesh):
    body = shards
    if mesh.shape["ep"] == 8 and mesh.shape["section"] == 4:
        body = fused
    placed = (
        P("ep", "section"),
        P("ep", "section"),
        P("ep", None),
        P("ep", None),
        P("ep", None, "section"),
        P("ep", None, "section"),
        P("ep", "section", None),
    )
    return jax.shard_map(
        body,
        mesh=mesh,
        in_specs=placed,
        out_specs=(P("ep", None, "section"), P("ep", None, "section"), P("ep", "section", None)),
        check_vma=False,
    )
```

```python
import jax
import jax.numpy as jnp
from jax import lax
from jax.experimental import pallas as pl
from jax.experimental.pallas import tpu as pltpu
from jax.sharding import PartitionSpec as P


def rounded(value):
    return lax.optimization_barrier(value.astype(jnp.bfloat16)).astype(jnp.float32)


def slot_grads(inputs, scaled, gate_w, up_w, down_w):
    gate = jnp.einsum("hpscd,sdf->hpscf", inputs, gate_w, preferred_element_type=jnp.float32)
    linear = jnp.einsum("hpscd,sdf->hpscf", inputs, up_w, preferred_element_type=jnp.float32)
    sigma = jax.nn.sigmoid(gate)
    hidden = (gate * sigma * linear).astype(jnp.bfloat16)
    grad_hidden = jnp.einsum("hpscd,sfd->hpscf", scaled, down_w, preferred_element_type=jnp.float32)
    gate_term = (grad_hidden * linear * sigma * (1.0 + gate * (1.0 - sigma))).astype(jnp.bfloat16)
    linear_term = (grad_hidden * gate * sigma).astype(jnp.bfloat16)
    part_gate = rounded(
        jnp.einsum("hpscd,hpscf->hsdf", inputs, gate_term, preferred_element_type=jnp.float32)
    )
    part_up = rounded(
        jnp.einsum("hpscd,hpscf->hsdf", inputs, linear_term, preferred_element_type=jnp.float32)
    )
    part_down = rounded(
        jnp.einsum("hpscf,hpscd->hsfd", hidden, scaled, preferred_element_type=jnp.float32)
    )
    return (part_gate, part_up, part_down)


def shards(tokens, grad_out, expert_ids, probs, w_gate, w_up, w_down):
    n_ep = lax.axis_size("ep")
    half = n_ep // 2
    tok_dev, top = expert_ids.shape
    picks = tok_dev * top
    capacity = max(2, (3 * picks + 2 * n_ep - 1) // (2 * n_ep))
    flat_ids = expert_ids.reshape(picks)
    owners = jnp.arange(n_ep, dtype=jnp.int32)
    slots = 1
    matches = (flat_ids[:, None] == owners[None, :]).astype(jnp.int32)
    rank = jnp.sum(jnp.cumsum(matches, axis=0) * matches, axis=1) - 1
    position = flat_ids * slots * capacity + rank
    width = tokens.shape[1]
    rows = jnp.repeat(tokens, top, axis=0)
    scaled = (
        probs.reshape(picks, 1) * jnp.repeat(grad_out, top, axis=0).astype(jnp.float32)
    ).astype(jnp.bfloat16)
    buffer_rows = n_ep * slots * capacity
    send_rows = jnp.zeros((buffer_rows, width), jnp.bfloat16).at[position].set(rows)
    send_scaled = jnp.zeros((buffer_rows, width), jnp.bfloat16).at[position].set(scaled)
    send_rows = send_rows.reshape(n_ep, slots * capacity, width)
    send_scaled = send_scaled.reshape(n_ep, slots * capacity, width)
    got_rows, got_scaled = (
        lax.all_to_all(send_rows, "ep", split_axis=0, concat_axis=0, tiled=True),
        lax.all_to_all(send_scaled, "ep", split_axis=0, concat_axis=0, tiled=True),
    )
    got_rows = got_rows.reshape(2, half, slots, capacity, width)
    got_scaled = got_scaled.reshape(2, half, slots, capacity, width)
    inputs, scaled_rows = (
        lax.all_gather(got_rows, "section", axis=4, tiled=True),
        lax.all_gather(got_scaled, "section", axis=4, tiled=True),
    )
    part_gate, part_up, part_down = slot_grads(inputs, scaled_rows, w_gate, w_up, w_down)
    grad_gate = (part_gate[0] + part_gate[1]).astype(jnp.bfloat16)
    grad_up = (part_up[0] + part_up[1]).astype(jnp.bfloat16)
    grad_down = (part_down[0] + part_down[1]).astype(jnp.bfloat16)
    return (grad_gate, grad_up, grad_down)


MESH = pl.DeviceIdType.MESH
TILE = 256


def fused_kernel(
    tokens, grad_out, ids, probs, w_gate, w_up, w_down,
    out_gate, out_up, out_down, out_in, out_scaled, out_term_gate, out_term_linear, out_term_hidden,
    held, wg, wu, wd, wg_t, wu_t, acc_gate, acc_up, acc_down, cols_in, cols_scaled, term_gate, term_linear, term_hidden,
    part_gate, part_up, part_down, out_sem, w_sem, z_send, z_recv, x_send, x_recv, y_send, y_recv, dx_send, dx_recv, dy_send, dy_recv, c_send, c_recv, d_send, d_recv,
):
    sec, me = lax.axis_index("section"), lax.axis_index("ep")
    width, n_tok = tokens.shape
    n_sec = held.shape[1]
    feats, units = w_gate.shape
    z, y = me // 2, me % 2
    h = z // 2
    zz = z + h * (3 - 2 * z)
    x_peer = (sec + 2) % 4
    core_peer = sec + 1 - 2 * (sec % 2)
    y_peer = me + 1 - 2 * y
    inward = me + 2 - 4 * h
    outward = me - 2 + 4 * h
    block_rows = held.shape[2]
    half = block_rows // 2
    side = block_rows // 5 // 16 * 16
    along = block_rows - 2 * side

    loads = [
        pltpu.make_async_copy(src, dst, w_sem.at[i])
        for i, (src, dst) in enumerate(((w_gate, wg), (w_up, wu), (w_down, wd)))
    ]
    for load in loads:
        load.start()

    barrier = pltpu.get_barrier_semaphore()

    def greet(**where):
        pl.semaphore_signal(barrier, inc=1, device_id=where, device_id_type=MESH)

    greet(section=x_peer)
    greet(section=core_peer)
    greet(ep=y_peer)
    greet(ep=inward)

    @pl.when(zz == 1)
    def _():
        greet(ep=outward)

    own = held.at[me, sec]
    own[:width, :] = tokens[...]
    own[width : 2 * width, :] = grad_out[...]
    n_ep = held.shape[0]
    expert = lax.broadcasted_iota(jnp.int32, (n_ep, n_tok), 0)
    weight = jnp.zeros((n_ep, n_tok), jnp.float32)
    for k in range(ids.shape[0]):
        weight = weight + jnp.where(ids[k : k + 1, :] == expert, probs[k : k + 1, :], 0.0)
    high = weight.astype(jnp.bfloat16).astype(jnp.float32)
    own[2 * width :, :] = jnp.concatenate([high, weight - high], axis=0).astype(jnp.bfloat16)

    @pl.when(zz == 0)
    def _():
        pl.semaphore_wait(barrier, 4)

    @pl.when(zz == 1)
    def _():
        pl.semaphore_wait(barrier, 5)

    def send(block, send_sem, recv_sem, **where):
        return pltpu.make_async_remote_copy(
            src_ref=block, dst_ref=block, send_sem=send_sem, recv_sem=recv_sem,
            device_id=where, device_id_type=MESH,
        )

    def source(k):
        s = k + (1 - k // 2) * ((k + zz) % 2 - k % 2)
        return s + h * (3 - 2 * s)

    def mine(k):
        return 2 * source(k) + y

    def other(k):
        return 2 * source(k) + 1 - y

    def upper(block, first):
        return block.at[pl.ds(0, half)] if first else block.at[pl.ds(along, side)]

    def lower(block, first):
        return block.at[pl.ds(half, half)] if first else block.at[pl.ds(along + side, side)]

    def d_block(k):
        return held.at[other(k), x_peer, pl.ds(0, along)]

    def d_in(k, idx):
        return send(d_block(k), d_send.at[0, idx], d_recv.at[idx], ep=inward)

    def d_out(k, idx):
        return send(d_block(k), d_send.at[1, idx], d_recv.at[idx], ep=outward)

    def d_arrived(k):
        send(d_block(k), d_send.at[0, k], d_recv.at[k], ep=inward).wait_recv()

    def z_arrived(k):
        send(held.at[mine(k), sec], z_send.at[0, k], z_recv.at[k], ep=inward).wait_recv()

    def z_in(k, idx):
        return send(held.at[mine(k), sec], z_send.at[0, idx], z_recv.at[idx], ep=inward)

    def z_out(k, idx):
        return send(held.at[mine(k), sec], z_send.at[1, idx], z_recv.at[idx], ep=outward)

    def x_whole(k):
        return send(held.at[mine(k), sec], x_send.at[k], x_recv.at[k], section=x_peer)

    def y_whole(k):
        return send(held.at[mine(k), sec], y_send.at[k], y_recv.at[k], ep=y_peer)

    def x_half(k, first):
        return send(upper(held.at[other(k), sec], first), dx_send.at[k], dx_recv.at[k], section=x_peer)

    def y_half(k, first):
        return send(lower(held.at[mine(k), x_peer], first), dy_send.at[k], dy_recv.at[k], ep=y_peer)

    def by_step(k, act):
        @pl.when(k == 0)
        def _():
            act(True)

        @pl.when(k > 0)
        def _():
            act(False)

    def core(k, which):
        block = held.at[mine(k) if which < 2 else other(k), sec if which % 2 == 0 else x_peer]
        return send(block, c_send.at[k, which], c_recv.at[k, which], section=core_peer)

    def x_arrived(k):
        send(held.at[mine(k), x_peer], x_send.at[k], x_recv.at[k], section=x_peer).wait_recv()

    def y_arrived(k):
        send(held.at[other(k), sec], y_send.at[k], y_recv.at[k], ep=y_peer).wait_recv()

    def diagonal_arrived(k):
        block = held.at[other(k), x_peer]

        def sides(first):
            send(upper(block, first), dx_send.at[k], dx_recv.at[k], section=x_peer).wait_recv()
            send(lower(block, first), dy_send.at[k], dy_recv.at[k], ep=y_peer).wait_recv()

        by_step(k, sides)

        @pl.when((zz == 0) & (k > 0))
        def _():
            d_arrived(k)

    def core_arrived(k, which):
        block = held.at[
            mine(k) if which < 2 else other(k),
            core_peer if which % 2 == 0 else (core_peer + 2) % 4,
        ]
        send(block, c_send.at[k, which], c_recv.at[k, which], section=core_peer).wait_recv()

    def column(k):
        x_whole(k).start()
        y_whole(k).start()
        core(k, 0).start()

    def forward(slot, at):
        here = pl.ds(at, n_tok)
        block = held.at[slot]
        parts = block[0, 2 * width :, :].astype(jnp.float32)
        which = lax.broadcasted_iota(jnp.int32, parts.shape, 0) % n_ep
        weight = jnp.sum(jnp.where(which == me, parts, 0.0), axis=0, keepdims=True)
        for s in range(n_sec):
            part = pl.ds(s * width, width)
            cols_in[part, here] = block[s, :width, :]
            cot = block[s, width : 2 * width, :].astype(jnp.float32)
            cols_scaled[part, here] = (weight * cot).astype(jnp.bfloat16)
        gate = jnp.dot(wg_t[...], cols_in[:, here], preferred_element_type=jnp.float32)
        linear = jnp.dot(wu_t[...], cols_in[:, here], preferred_element_type=jnp.float32)
        grad = jnp.dot(wd[...], cols_scaled[:, here], preferred_element_type=jnp.float32)
        sigma = jax.nn.sigmoid(gate)
        silu = gate * sigma
        term_hidden[:, here] = (silu * linear).astype(jnp.bfloat16)
        term_gate[:, here] = (grad * linear * sigma * (1.0 + gate * (1.0 - sigma))).astype(jnp.bfloat16)
        term_linear[:, here] = (grad * silu).astype(jnp.bfloat16)

    def outer(lhs, rhs):
        return lax.dot_general(lhs, rhs, (((1,), (1,)), ((), ())), preferred_element_type=jnp.float32)

    products = (
        (acc_gate, part_gate, cols_in, term_gate, units),
        (acc_up, part_up, cols_in, term_linear, units),
        (acc_down, part_down, term_hidden, cols_scaled, feats),
    )

    def first_weights():
        for acc, _, lhs, rhs, size in products:
            for at in range(0, size, TILE):
                to = min(size, at + TILE)
                acc[:, at:to] = outer(lhs[...], rhs[at:to, :])

    def second_weights():
        both = 2 * n_tok
        for acc, part, lhs, rhs, size in products:
            for at in range(0, size, TILE):
                to = min(size, at + TILE)
                part[:, at:to] = (acc[:, at:to] + outer(lhs[:, :both], rhs[at:to, :both])).astype(jnp.bfloat16)

    z_in(0, 1 + zz).start()

    @pl.when(zz == 1)
    def _():
        z_out(0, 1).start()

    column(0)

    for load in loads:
        load.wait()
    for at in range(0, feats, TILE):
        to = min(feats, at + TILE)
        wg_t[:, at:to] = wg[at:to, :].T
        wu_t[:, at:to] = wu[at:to, :].T

    pairs = (
        (part_gate, out_gate), (part_up, out_up), (part_down, out_down), (cols_in, out_in), (cols_scaled, out_scaled),
        (term_gate, out_term_gate), (term_linear, out_term_linear), (term_hidden, out_term_hidden),
    )
    results = [pltpu.make_async_copy(src, dst, out_sem.at[i]) for i, (src, dst) in enumerate(pairs)]

    def step(k, carry):
        x_arrived(k)
        by_step(k, lambda first: y_half(k, first).start())
        core(k, 1).start()
        y_arrived(k)
        by_step(k, lambda first: x_half(k, first).start())
        core(k, 2).start()

        @pl.when(k == 0)
        def _():
            z_arrived(1)

            @pl.when(zz == 1)
            def _():
                z_in(1, 3).start()
                z_arrived(2)
                z_out(2, 2).start()

            column(1)

        core_arrived(k, 0)
        core_arrived(k, 1)
        forward(mine(k), pl.multiple_of((1 - (k + 3) // 4) * 2 * n_tok, n_tok))

        @pl.when(k == 0)
        def _():
            diagonal_arrived(0)
            core(0, 3).start()
            d_in(0, 1 + zz).start()

            @pl.when(zz == 1)
            def _():
                d_out(0, 1).start()
                z_arrived(3)
                z_out(3, 3).start()

            @pl.when(zz == 0)
            def _():
                z_arrived(2)

            column(2)

        @pl.when((zz == 1) & (k == 1))
        def _():
            d_arrived(1)
            d_in(1, 3).start()
            d_arrived(2)
            d_out(2, 2).start()

        @pl.when(k > 0)
        def _():
            core_arrived(k - 1, 2)
            core_arrived(k - 1, 3)
            forward(other(k - 1), n_tok)

        @pl.when(k == 1)
        def _():
            @pl.when(zz == 0)
            def _():
                z_arrived(3)

            column(3)
            first_weights()

            @pl.when(zz == 1)
            def _():
                d_arrived(3)
                d_out(3, 3).start()

        @pl.when(k == 2)
        def _():
            second_weights()
            for result in results[:3]:
                result.start()

        @pl.when(k > 0)
        def _():
            diagonal_arrived(k)
            core(k, 3).start()

        return carry

    lax.fori_loop(0, 4, step, 0)
    core_arrived(3, 2)
    core_arrived(3, 3)
    forward(other(3), 2 * n_tok)

    for result in results[3:]:
        result.start()
    z_in(0, 1 + zz).wait_send()
    d_in(0, 1 + zz).wait_send()

    @pl.when(zz == 1)
    def _():
        z_out(0, 1).wait_send()
        z_in(1, 3).wait_send()
        z_out(2, 2).wait_send()
        z_out(3, 3).wait_send()
        d_out(0, 1).wait_send()
        d_in(1, 3).wait_send()
        d_out(2, 2).wait_send()
        d_out(3, 3).wait_send()

    def drain(k, carry):
        x_whole(k).wait_send()
        y_whole(k).wait_send()

        def sides(first):
            x_half(k, first).wait_send()
            y_half(k, first).wait_send()

        by_step(k, sides)
        for which in range(4):
            core(k, which).wait_send()
        return carry

    lax.fori_loop(0, 4, drain, 0)
    for result in results:
        result.wait()


def last_kernel(
    part_gate, part_up, part_down, cols_in, cols_scaled, term_gate, term_linear, term_hidden, out_gate, out_up, out_down
):
    def outer(lhs, rhs):
        return lax.dot_general(lhs, rhs, (((1,), (1,)), ((), ())), preferred_element_type=jnp.float32)

    for part, out, lhs, rhs in (
        (part_gate, out_gate, cols_in, term_gate),
        (part_up, out_up, cols_in, term_linear),
        (part_down, out_down, term_hidden, cols_scaled),
    ):
        out[...] = (part[...].astype(jnp.float32) + outer(lhs[...], rhs[...])).astype(jnp.bfloat16)


def fused(tokens, grad_out, expert_ids, probs, w_gate, w_up, w_down):
    n_ep, n_sec = lax.axis_size("ep"), lax.axis_size("section")
    n_tok, width = tokens.shape
    feats, units = w_gate.shape[1:]
    bf16, f32 = jnp.bfloat16, jnp.float32
    dma = pltpu.SemaphoreType.DMA
    vmem, hbm = pl.BlockSpec(memory_space=pltpu.VMEM), pl.BlockSpec(memory_space=pl.ANY)
    rows = n_ep * n_tok
    shapes = (
        jax.ShapeDtypeStruct((feats, units), bf16),
        jax.ShapeDtypeStruct((feats, units), bf16),
        jax.ShapeDtypeStruct((units, feats), bf16),
    )
    outs = pl.pallas_call(
        fused_kernel,
        out_shape=shapes
        + tuple(jax.ShapeDtypeStruct((size, 3 * n_tok), bf16) for size in (feats, feats, units, units, units)),
        in_specs=[vmem] * 4 + [hbm] * 3,
        out_specs=(hbm,) * 8,
        scratch_shapes=[
            pltpu.VMEM((n_ep, n_sec, 2 * width + 2 * n_ep, n_tok), bf16),
            pltpu.VMEM((feats, units), bf16),
            pltpu.VMEM((feats, units), bf16),
            pltpu.VMEM((units, feats), bf16),
            pltpu.VMEM((units, feats), bf16),
            pltpu.VMEM((units, feats), bf16),
            pltpu.VMEM((feats, units), f32),
            pltpu.VMEM((feats, units), f32),
            pltpu.VMEM((units, feats), f32),
            pltpu.VMEM((feats, 3 * n_tok), bf16),
            pltpu.VMEM((feats, 3 * n_tok), bf16),
            pltpu.VMEM((units, 3 * n_tok), bf16),
            pltpu.VMEM((units, 3 * n_tok), bf16),
            pltpu.VMEM((units, 3 * n_tok), bf16),
            pltpu.VMEM((feats, units), bf16),
            pltpu.VMEM((feats, units), bf16),
            pltpu.VMEM((units, feats), bf16),
            dma((8,)),
            dma((3,)),
            dma((2, 4)), dma((4,)),
            dma((4,)), dma((4,)), dma((4,)), dma((4,)),
            dma((4,)), dma((4,)), dma((4,)), dma((4,)),
            dma((4, 4)), dma((4, 4)),
            dma((2, 4)), dma((4,)),
        ],
        cost_estimate=pl.CostEstimate(
            flops=12 * rows * feats * units, bytes_accessed=12 * feats * units, transcendentals=rows * units
        ),
        compiler_params=pltpu.CompilerParams(
            collective_id=0, has_side_effects=True, vmem_limit_bytes=60 * 1024 * 1024
        ),
    )(tokens.T, grad_out.T, expert_ids.T, probs.T, w_gate[0], w_up[0], w_down[0])
    steps = 5

    def by_rows(size, other):
        return pl.BlockSpec((size // steps, other), lambda i: (i, 0))

    def whole(size):
        return pl.BlockSpec((size, 3 * n_tok), lambda i: (0, 0))

    blocks = [by_rows(feats, units), by_rows(feats, units), by_rows(units, feats)]
    outs = pl.pallas_call(
        last_kernel,
        out_shape=shapes,
        grid=(steps,),
        in_specs=blocks
        + [by_rows(feats, 3 * n_tok), whole(feats), whole(units), whole(units), by_rows(units, 3 * n_tok)],
        out_specs=tuple(blocks),
        cost_estimate=pl.CostEstimate(
            flops=18 * n_tok * feats * units, bytes_accessed=12 * feats * units, transcendentals=0
        ),
        compiler_params=pltpu.CompilerParams(vmem_limit_bytes=60 * 1024 * 1024),
    )(*outs)
    return tuple(out[None] for out in outs)


def solution(mesh):
    body = shards
    if mesh.shape["ep"] == 8 and mesh.shape["section"] == 4:
        body = fused
    placed = (
        P("ep", "section"),
        P("ep", "section"),
        P("ep", None),
        P("ep", None),
        P("ep", None, "section"),
        P("ep", None, "section"),
        P("ep", "section", None),
    )
    return jax.shard_map(
        body,
        mesh=mesh,
        in_specs=placed,
        out_specs=(P("ep", None, "section"), P("ep", None, "section"), P("ep", "section", None)),
        check_vma=False,
    )
```

```python
import jax
import jax.numpy as jnp
from jax import lax
from jax.experimental import pallas as pl
from jax.experimental.pallas import tpu as pltpu
from jax.sharding import PartitionSpec as P


def rounded(value):
    return lax.optimization_barrier(value.astype(jnp.bfloat16)).astype(jnp.float32)


def slot_grads(inputs, scaled, gate_w, up_w, down_w):
    gate = jnp.einsum("hpscd,sdf->hpscf", inputs, gate_w, preferred_element_type=jnp.float32)
    linear = jnp.einsum("hpscd,sdf->hpscf", inputs, up_w, preferred_element_type=jnp.float32)
    sigma = jax.nn.sigmoid(gate)
    hidden = (gate * sigma * linear).astype(jnp.bfloat16)
    grad_hidden = jnp.einsum("hpscd,sfd->hpscf", scaled, down_w, preferred_element_type=jnp.float32)
    gate_term = (grad_hidden * linear * sigma * (1.0 + gate * (1.0 - sigma))).astype(jnp.bfloat16)
    linear_term = (grad_hidden * gate * sigma).astype(jnp.bfloat16)
    part_gate = rounded(
        jnp.einsum("hpscd,hpscf->hsdf", inputs, gate_term, preferred_element_type=jnp.float32)
    )
    part_up = rounded(
        jnp.einsum("hpscd,hpscf->hsdf", inputs, linear_term, preferred_element_type=jnp.float32)
    )
    part_down = rounded(
        jnp.einsum("hpscf,hpscd->hsfd", hidden, scaled, preferred_element_type=jnp.float32)
    )
    return (part_gate, part_up, part_down)


def shards(tokens, grad_out, expert_ids, probs, w_gate, w_up, w_down):
    n_ep = lax.axis_size("ep")
    half = n_ep // 2
    tok_dev, top = expert_ids.shape
    picks = tok_dev * top
    capacity = max(2, (3 * picks + 2 * n_ep - 1) // (2 * n_ep))
    flat_ids = expert_ids.reshape(picks)
    owners = jnp.arange(n_ep, dtype=jnp.int32)
    slots = 1
    matches = (flat_ids[:, None] == owners[None, :]).astype(jnp.int32)
    rank = jnp.sum(jnp.cumsum(matches, axis=0) * matches, axis=1) - 1
    position = flat_ids * slots * capacity + rank
    width = tokens.shape[1]
    rows = jnp.repeat(tokens, top, axis=0)
    scaled = (
        probs.reshape(picks, 1) * jnp.repeat(grad_out, top, axis=0).astype(jnp.float32)
    ).astype(jnp.bfloat16)
    buffer_rows = n_ep * slots * capacity
    send_rows = jnp.zeros((buffer_rows, width), jnp.bfloat16).at[position].set(rows)
    send_scaled = jnp.zeros((buffer_rows, width), jnp.bfloat16).at[position].set(scaled)
    send_rows = send_rows.reshape(n_ep, slots * capacity, width)
    send_scaled = send_scaled.reshape(n_ep, slots * capacity, width)
    got_rows, got_scaled = (
        lax.all_to_all(send_rows, "ep", split_axis=0, concat_axis=0, tiled=True),
        lax.all_to_all(send_scaled, "ep", split_axis=0, concat_axis=0, tiled=True),
    )
    got_rows = got_rows.reshape(2, half, slots, capacity, width)
    got_scaled = got_scaled.reshape(2, half, slots, capacity, width)
    inputs, scaled_rows = (
        lax.all_gather(got_rows, "section", axis=4, tiled=True),
        lax.all_gather(got_scaled, "section", axis=4, tiled=True),
    )
    part_gate, part_up, part_down = slot_grads(inputs, scaled_rows, w_gate, w_up, w_down)
    grad_gate = (part_gate[0] + part_gate[1]).astype(jnp.bfloat16)
    grad_up = (part_up[0] + part_up[1]).astype(jnp.bfloat16)
    grad_down = (part_down[0] + part_down[1]).astype(jnp.bfloat16)
    return (grad_gate, grad_up, grad_down)


MESH = pl.DeviceIdType.MESH
TILE = 256


def fused_kernel(
    tokens, grad_out, ids, probs, w_gate, w_up, w_down,
    out_gate, out_up, out_down, out_in, out_scaled, out_term_gate, out_term_linear, out_term_hidden,
    held, wg, wu, wd, wg_t, wu_t, acc_gate, acc_up, acc_down, cols_in, cols_scaled, term_gate, term_linear, term_hidden,
    part_gate, part_up, part_down, out_sem, w_sem, z_send, z_recv, x_send, x_recv, y_send, y_recv, dx_send, dx_recv, dy_send, dy_recv, c_send, c_recv, d_send, d_recv,
):
    sec, me = lax.axis_index("section"), lax.axis_index("ep")
    width, n_tok = tokens.shape
    n_sec = held.shape[1]
    feats, units = w_gate.shape
    z, y = me // 2, me % 2
    h = z // 2
    zz = z + h * (3 - 2 * z)
    x_peer = (sec + 2) % 4
    core_peer = sec + 1 - 2 * (sec % 2)
    y_peer = me + 1 - 2 * y
    inward = me + 2 - 4 * h
    outward = me - 2 + 4 * h
    block_rows = held.shape[2]
    half = block_rows // 2
    side = block_rows // 5 // 16 * 16
    along = block_rows - 2 * side

    loads = [
        pltpu.make_async_copy(src, dst, w_sem.at[i])
        for i, (src, dst) in enumerate(((w_gate, wg), (w_up, wu), (w_down, wd)))
    ]
    for load in loads:
        load.start()

    barrier = pltpu.get_barrier_semaphore()

    def greet(**where):
        pl.semaphore_signal(barrier, inc=1, device_id=where, device_id_type=MESH)

    greet(section=x_peer)
    greet(section=core_peer)
    greet(ep=y_peer)
    greet(ep=inward)

    @pl.when(zz == 1)
    def _():
        greet(ep=outward)

    own = held.at[me, sec]
    own[:width, :] = tokens[...]
    own[width : 2 * width, :] = grad_out[...]
    n_ep = held.shape[0]
    expert = lax.broadcasted_iota(jnp.int32, (n_ep, n_tok), 0)
    weight = jnp.zeros((n_ep, n_tok), jnp.float32)
    for k in range(ids.shape[0]):
        weight = weight + jnp.where(ids[k : k + 1, :] == expert, probs[k : k + 1, :], 0.0)
    high = weight.astype(jnp.bfloat16).astype(jnp.float32)
    own[2 * width :, :] = jnp.concatenate([high, weight - high], axis=0).astype(jnp.bfloat16)

    @pl.when(zz == 0)
    def _():
        pl.semaphore_wait(barrier, 4)

    @pl.when(zz == 1)
    def _():
        pl.semaphore_wait(barrier, 5)

    def send(block, send_sem, recv_sem, **where):
        return pltpu.make_async_remote_copy(
            src_ref=block, dst_ref=block, send_sem=send_sem, recv_sem=recv_sem,
            device_id=where, device_id_type=MESH,
        )

    def source(k):
        s = k + (1 - k // 2) * ((k + zz) % 2 - k % 2)
        return s + h * (3 - 2 * s)

    def mine(k):
        return 2 * source(k) + y

    def other(k):
        return 2 * source(k) + 1 - y

    def upper(block, first):
        return block.at[pl.ds(0, half)] if first else block.at[pl.ds(along, side)]

    def lower(block, first):
        return block.at[pl.ds(half, half)] if first else block.at[pl.ds(along + side, side)]

    def d_block(k):
        return held.at[other(k), x_peer, pl.ds(0, along)]

    def d_in(k, idx):
        return send(d_block(k), d_send.at[0, idx], d_recv.at[idx], ep=inward)

    def d_out(k, idx):
        return send(d_block(k), d_send.at[1, idx], d_recv.at[idx], ep=outward)

    def d_arrived(k):
        send(d_block(k), d_send.at[0, k], d_recv.at[k], ep=inward).wait_recv()

    def z_arrived(k):
        send(held.at[mine(k), sec], z_send.at[0, k], z_recv.at[k], ep=inward).wait_recv()

    def z_in(k, idx):
        return send(held.at[mine(k), sec], z_send.at[0, idx], z_recv.at[idx], ep=inward)

    def z_out(k, idx):
        return send(held.at[mine(k), sec], z_send.at[1, idx], z_recv.at[idx], ep=outward)

    def x_whole(k):
        return send(held.at[mine(k), sec], x_send.at[k], x_recv.at[k], section=x_peer)

    def y_whole(k):
        return send(held.at[mine(k), sec], y_send.at[k], y_recv.at[k], ep=y_peer)

    def x_half(k, first):
        return send(upper(held.at[other(k), sec], first), dx_send.at[k], dx_recv.at[k], section=x_peer)

    def y_half(k, first):
        return send(lower(held.at[mine(k), x_peer], first), dy_send.at[k], dy_recv.at[k], ep=y_peer)

    def by_step(k, act):
        @pl.when(k == 0)
        def _():
            act(True)

        @pl.when(k > 0)
        def _():
            act(False)

    def core(k, which):
        block = held.at[mine(k) if which < 2 else other(k), sec if which % 2 == 0 else x_peer]
        return send(block, c_send.at[k, which], c_recv.at[k, which], section=core_peer)

    def x_arrived(k):
        send(held.at[mine(k), x_peer], x_send.at[k], x_recv.at[k], section=x_peer).wait_recv()

    def y_arrived(k):
        send(held.at[other(k), sec], y_send.at[k], y_recv.at[k], ep=y_peer).wait_recv()

    def diagonal_arrived(k):
        block = held.at[other(k), x_peer]

        def sides(first):
            send(upper(block, first), dx_send.at[k], dx_recv.at[k], section=x_peer).wait_recv()
            send(lower(block, first), dy_send.at[k], dy_recv.at[k], ep=y_peer).wait_recv()

        by_step(k, sides)

        @pl.when((zz == 0) & (k > 0))
        def _():
            d_arrived(k)

    def core_arrived(k, which):
        block = held.at[
            mine(k) if which < 2 else other(k),
            core_peer if which % 2 == 0 else (core_peer + 2) % 4,
        ]
        send(block, c_send.at[k, which], c_recv.at[k, which], section=core_peer).wait_recv()

    def column(k):
        x_whole(k).start()
        y_whole(k).start()
        core(k, 0).start()

    def forward(slot, at):
        here = pl.ds(at, n_tok)
        block = held.at[slot]
        parts = block[0, 2 * width :, :].astype(jnp.float32)
        which = lax.broadcasted_iota(jnp.int32, parts.shape, 0) % n_ep
        weight = jnp.sum(jnp.where(which == me, parts, 0.0), axis=0, keepdims=True)
        for s in range(n_sec):
            part = pl.ds(s * width, width)
            cols_in[part, here] = block[s, :width, :]
            cot = block[s, width : 2 * width, :].astype(jnp.float32)
            cols_scaled[part, here] = (weight * cot).astype(jnp.bfloat16)
        gate = jnp.dot(wg_t[...], cols_in[:, here], preferred_element_type=jnp.float32)
        linear = jnp.dot(wu_t[...], cols_in[:, here], preferred_element_type=jnp.float32)
        grad = jnp.dot(wd[...], cols_scaled[:, here], preferred_element_type=jnp.float32)
        sigma = jax.nn.sigmoid(gate)
        silu = gate * sigma
        term_hidden[:, here] = (silu * linear).astype(jnp.bfloat16)
        term_gate[:, here] = (grad * linear * sigma * (1.0 + gate * (1.0 - sigma))).astype(jnp.bfloat16)
        term_linear[:, here] = (grad * silu).astype(jnp.bfloat16)

    def outer(lhs, rhs):
        return lax.dot_general(lhs, rhs, (((1,), (1,)), ((), ())), preferred_element_type=jnp.float32)

    products = (
        (acc_gate, part_gate, cols_in, term_gate, units),
        (acc_up, part_up, cols_in, term_linear, units),
        (acc_down, part_down, term_hidden, cols_scaled, feats),
    )

    def first_weights():
        for acc, _, lhs, rhs, size in products:
            for at in range(0, size, TILE):
                to = min(size, at + TILE)
                acc[:, at:to] = outer(lhs[...], rhs[at:to, :])

    def second_weights():
        for acc, part, lhs, rhs, size in products:
            for at in range(0, size, TILE):
                to = min(size, at + TILE)
                part[:, at:to] = (acc[:, at:to] + outer(lhs[...], rhs[at:to, :])).astype(jnp.bfloat16)

    z_in(0, 1 + zz).start()

    @pl.when(zz == 1)
    def _():
        z_out(0, 1).start()

    column(0)

    for load in loads:
        load.wait()
    for at in range(0, feats, TILE):
        to = min(feats, at + TILE)
        wg_t[:, at:to] = wg[at:to, :].T
        wu_t[:, at:to] = wu[at:to, :].T

    pairs = (
        (part_gate, out_gate), (part_up, out_up), (part_down, out_down), (cols_in, out_in), (cols_scaled, out_scaled),
        (term_gate, out_term_gate), (term_linear, out_term_linear), (term_hidden, out_term_hidden),
    )
    results = [
        pltpu.make_async_copy(src if i < 3 else src.at[:, pl.ds(0, 2 * n_tok)], dst, out_sem.at[i])
        for i, (src, dst) in enumerate(pairs)
    ]

    def step(k, carry):
        x_arrived(k)
        by_step(k, lambda first: y_half(k, first).start())
        core(k, 1).start()
        y_arrived(k)
        by_step(k, lambda first: x_half(k, first).start())
        core(k, 2).start()

        @pl.when(k == 0)
        def _():
            z_arrived(1)

            @pl.when(zz == 1)
            def _():
                z_in(1, 3).start()
                z_arrived(2)
                z_out(2, 2).start()

            column(1)

        core_arrived(k, 0)
        core_arrived(k, 1)
        forward(mine(k), pl.multiple_of((1 - (k + 3) // 4) * 2 * n_tok, n_tok))

        @pl.when(k == 0)
        def _():
            diagonal_arrived(0)
            core(0, 3).start()
            d_in(0, 1 + zz).start()

            @pl.when(zz == 1)
            def _():
                d_out(0, 1).start()
                z_arrived(3)
                z_out(3, 3).start()

            @pl.when(zz == 0)
            def _():
                z_arrived(2)

            column(2)

        @pl.when((zz == 1) & (k == 1))
        def _():
            d_arrived(1)
            d_in(1, 3).start()
            d_arrived(2)
            d_out(2, 2).start()

        @pl.when((k == 1) | (k == 2))
        def _():
            core_arrived(k - 1, 2)
            core_arrived(k - 1, 3)
            forward(other(k - 1), n_tok)

        @pl.when(k == 1)
        def _():
            @pl.when(zz == 0)
            def _():
                z_arrived(3)

            column(3)
            first_weights()

            @pl.when(zz == 1)
            def _():
                d_arrived(3)
                d_out(3, 3).start()

        @pl.when(k > 0)
        def _():
            diagonal_arrived(k)
            core(k, 3).start()

        @pl.when(k == 2)
        def _():
            core_arrived(2, 2)
            core_arrived(2, 3)
            forward(other(2), 2 * n_tok)
            second_weights()
            for result in results[:3]:
                result.start()

        return carry

    lax.fori_loop(0, 4, step, 0)
    core_arrived(3, 2)
    core_arrived(3, 3)
    forward(other(3), n_tok)

    for result in results[3:]:
        result.start()
    z_in(0, 1 + zz).wait_send()
    d_in(0, 1 + zz).wait_send()

    @pl.when(zz == 1)
    def _():
        z_out(0, 1).wait_send()
        z_in(1, 3).wait_send()
        z_out(2, 2).wait_send()
        z_out(3, 3).wait_send()
        d_out(0, 1).wait_send()
        d_in(1, 3).wait_send()
        d_out(2, 2).wait_send()
        d_out(3, 3).wait_send()

    def drain(k, carry):
        x_whole(k).wait_send()
        y_whole(k).wait_send()

        def sides(first):
            x_half(k, first).wait_send()
            y_half(k, first).wait_send()

        by_step(k, sides)
        for which in range(4):
            core(k, which).wait_send()
        return carry

    lax.fori_loop(0, 4, drain, 0)
    for result in results:
        result.wait()


def last_kernel(
    part_gate, part_up, part_down, cols_in, cols_scaled, term_gate, term_linear, term_hidden, out_gate, out_up, out_down
):
    def outer(lhs, rhs):
        return lax.dot_general(lhs, rhs, (((1,), (1,)), ((), ())), preferred_element_type=jnp.float32)

    for part, out, lhs, rhs in (
        (part_gate, out_gate, cols_in, term_gate),
        (part_up, out_up, cols_in, term_linear),
        (part_down, out_down, term_hidden, cols_scaled),
    ):
        out[...] = (part[...].astype(jnp.float32) + outer(lhs[...], rhs[...])).astype(jnp.bfloat16)


def fused(tokens, grad_out, expert_ids, probs, w_gate, w_up, w_down):
    n_ep, n_sec = lax.axis_size("ep"), lax.axis_size("section")
    n_tok, width = tokens.shape
    feats, units = w_gate.shape[1:]
    bf16, f32 = jnp.bfloat16, jnp.float32
    dma = pltpu.SemaphoreType.DMA
    vmem, hbm = pl.BlockSpec(memory_space=pltpu.VMEM), pl.BlockSpec(memory_space=pl.ANY)
    rows = n_ep * n_tok
    shapes = (
        jax.ShapeDtypeStruct((feats, units), bf16),
        jax.ShapeDtypeStruct((feats, units), bf16),
        jax.ShapeDtypeStruct((units, feats), bf16),
    )
    outs = pl.pallas_call(
        fused_kernel,
        out_shape=shapes
        + tuple(jax.ShapeDtypeStruct((size, 2 * n_tok), bf16) for size in (feats, feats, units, units, units)),
        in_specs=[vmem] * 4 + [hbm] * 3,
        out_specs=(hbm,) * 8,
        scratch_shapes=[
            pltpu.VMEM((n_ep, n_sec, 2 * width + 2 * n_ep, n_tok), bf16),
            pltpu.VMEM((feats, units), bf16),
            pltpu.VMEM((feats, units), bf16),
            pltpu.VMEM((units, feats), bf16),
            pltpu.VMEM((units, feats), bf16),
            pltpu.VMEM((units, feats), bf16),
            pltpu.VMEM((feats, units), f32),
            pltpu.VMEM((feats, units), f32),
            pltpu.VMEM((units, feats), f32),
            pltpu.VMEM((feats, 3 * n_tok), bf16),
            pltpu.VMEM((feats, 3 * n_tok), bf16),
            pltpu.VMEM((units, 3 * n_tok), bf16),
            pltpu.VMEM((units, 3 * n_tok), bf16),
            pltpu.VMEM((units, 3 * n_tok), bf16),
            pltpu.VMEM((feats, units), bf16),
            pltpu.VMEM((feats, units), bf16),
            pltpu.VMEM((units, feats), bf16),
            dma((8,)),
            dma((3,)),
            dma((2, 4)), dma((4,)),
            dma((4,)), dma((4,)), dma((4,)), dma((4,)),
            dma((4,)), dma((4,)), dma((4,)), dma((4,)),
            dma((4, 4)), dma((4, 4)),
            dma((2, 4)), dma((4,)),
        ],
        cost_estimate=pl.CostEstimate(
            flops=12 * rows * feats * units, bytes_accessed=12 * feats * units, transcendentals=rows * units
        ),
        compiler_params=pltpu.CompilerParams(
            collective_id=0, has_side_effects=True, vmem_limit_bytes=60 * 1024 * 1024
        ),
    )(tokens.T, grad_out.T, expert_ids.T, probs.T, w_gate[0], w_up[0], w_down[0])
    steps = 5

    def by_rows(size, other):
        return pl.BlockSpec((size // steps, other), lambda i: (i, 0))

    def whole(size):
        return pl.BlockSpec((size, 2 * n_tok), lambda i: (0, 0))

    blocks = [by_rows(feats, units), by_rows(feats, units), by_rows(units, feats)]
    outs = pl.pallas_call(
        last_kernel,
        out_shape=shapes,
        grid=(steps,),
        in_specs=blocks
        + [by_rows(feats, 2 * n_tok), whole(feats), whole(units), whole(units), by_rows(units, 2 * n_tok)],
        out_specs=tuple(blocks),
        cost_estimate=pl.CostEstimate(
            flops=12 * n_tok * feats * units, bytes_accessed=12 * feats * units, transcendentals=0
        ),
        compiler_params=pltpu.CompilerParams(vmem_limit_bytes=60 * 1024 * 1024),
    )(*outs)
    return tuple(out[None] for out in outs)


def solution(mesh):
    body = shards
    if mesh.shape["ep"] == 8 and mesh.shape["section"] == 4:
        body = fused
    placed = (
        P("ep", "section"),
        P("ep", "section"),
        P("ep", None),
        P("ep", None),
        P("ep", None, "section"),
        P("ep", None, "section"),
        P("ep", "section", None),
    )
    return jax.shard_map(
        body,
        mesh=mesh,
        in_specs=placed,
        out_specs=(P("ep", None, "section"), P("ep", None, "section"), P("ep", "section", None)),
        check_vma=False,
    )
```

```python
import jax
import jax.numpy as jnp
from jax import lax
from jax.experimental import pallas as pl
from jax.experimental.pallas import tpu as pltpu
from jax.sharding import PartitionSpec as P


def rounded(value):
    return lax.optimization_barrier(value.astype(jnp.bfloat16)).astype(jnp.float32)


def slot_grads(inputs, scaled, gate_w, up_w, down_w):
    gate = jnp.einsum("hpscd,sdf->hpscf", inputs, gate_w, preferred_element_type=jnp.float32)
    linear = jnp.einsum("hpscd,sdf->hpscf", inputs, up_w, preferred_element_type=jnp.float32)
    sigma = jax.nn.sigmoid(gate)
    hidden = (gate * sigma * linear).astype(jnp.bfloat16)
    grad_hidden = jnp.einsum("hpscd,sfd->hpscf", scaled, down_w, preferred_element_type=jnp.float32)
    gate_term = (grad_hidden * linear * sigma * (1.0 + gate * (1.0 - sigma))).astype(jnp.bfloat16)
    linear_term = (grad_hidden * gate * sigma).astype(jnp.bfloat16)
    part_gate = rounded(
        jnp.einsum("hpscd,hpscf->hsdf", inputs, gate_term, preferred_element_type=jnp.float32)
    )
    part_up = rounded(
        jnp.einsum("hpscd,hpscf->hsdf", inputs, linear_term, preferred_element_type=jnp.float32)
    )
    part_down = rounded(
        jnp.einsum("hpscf,hpscd->hsfd", hidden, scaled, preferred_element_type=jnp.float32)
    )
    return (part_gate, part_up, part_down)


def shards(tokens, grad_out, expert_ids, probs, w_gate, w_up, w_down):
    n_ep = lax.axis_size("ep")
    half = n_ep // 2
    tok_dev, top = expert_ids.shape
    picks = tok_dev * top
    capacity = max(2, (3 * picks + 2 * n_ep - 1) // (2 * n_ep))
    flat_ids = expert_ids.reshape(picks)
    owners = jnp.arange(n_ep, dtype=jnp.int32)
    slots = 1
    matches = (flat_ids[:, None] == owners[None, :]).astype(jnp.int32)
    rank = jnp.sum(jnp.cumsum(matches, axis=0) * matches, axis=1) - 1
    position = flat_ids * slots * capacity + rank
    width = tokens.shape[1]
    rows = jnp.repeat(tokens, top, axis=0)
    scaled = (
        probs.reshape(picks, 1) * jnp.repeat(grad_out, top, axis=0).astype(jnp.float32)
    ).astype(jnp.bfloat16)
    buffer_rows = n_ep * slots * capacity
    send_rows = jnp.zeros((buffer_rows, width), jnp.bfloat16).at[position].set(rows)
    send_scaled = jnp.zeros((buffer_rows, width), jnp.bfloat16).at[position].set(scaled)
    send_rows = send_rows.reshape(n_ep, slots * capacity, width)
    send_scaled = send_scaled.reshape(n_ep, slots * capacity, width)
    got_rows, got_scaled = (
        lax.all_to_all(send_rows, "ep", split_axis=0, concat_axis=0, tiled=True),
        lax.all_to_all(send_scaled, "ep", split_axis=0, concat_axis=0, tiled=True),
    )
    got_rows = got_rows.reshape(2, half, slots, capacity, width)
    got_scaled = got_scaled.reshape(2, half, slots, capacity, width)
    inputs, scaled_rows = (
        lax.all_gather(got_rows, "section", axis=4, tiled=True),
        lax.all_gather(got_scaled, "section", axis=4, tiled=True),
    )
    part_gate, part_up, part_down = slot_grads(inputs, scaled_rows, w_gate, w_up, w_down)
    grad_gate = (part_gate[0] + part_gate[1]).astype(jnp.bfloat16)
    grad_up = (part_up[0] + part_up[1]).astype(jnp.bfloat16)
    grad_down = (part_down[0] + part_down[1]).astype(jnp.bfloat16)
    return (grad_gate, grad_up, grad_down)


MESH = pl.DeviceIdType.MESH
TILE = 256


def fused_kernel(
    tokens, grad_out, ids, probs, w_gate, w_up, w_down,
    out_gate, out_up, out_down, out_in, out_scaled, out_term_gate, out_term_linear, out_term_hidden,
    held, wg, wu, wd, wg_t, wu_t, acc_gate, acc_up, acc_down, cols_in, cols_scaled, term_gate, term_linear, term_hidden,
    part_gate, part_up, part_down, out_sem, w_sem, z_send, z_recv, x_send, x_recv, y_send, y_recv, dx_send, dx_recv, dy_send, dy_recv, c_send, c_recv, d_send, d_recv,
):
    sec, me = lax.axis_index("section"), lax.axis_index("ep")
    width, n_tok = tokens.shape
    n_sec = held.shape[1]
    feats, units = w_gate.shape
    z, y = me // 2, me % 2
    h = z // 2
    zz = z + h * (3 - 2 * z)
    x_peer = (sec + 2) % 4
    core_peer = sec + 1 - 2 * (sec % 2)
    y_peer = me + 1 - 2 * y
    inward = me + 2 - 4 * h
    outward = me - 2 + 4 * h
    block_rows = held.shape[2]
    half = block_rows // 2
    side = block_rows // 5 // 16 * 16
    along = block_rows - 2 * side

    loads = [
        pltpu.make_async_copy(src, dst, w_sem.at[i])
        for i, (src, dst) in enumerate(((w_gate, wg), (w_up, wu), (w_down, wd)))
    ]
    for load in loads:
        load.start()

    barrier = pltpu.get_barrier_semaphore()

    def greet(**where):
        pl.semaphore_signal(barrier, inc=1, device_id=where, device_id_type=MESH)

    greet(section=x_peer)
    greet(section=core_peer)
    greet(ep=y_peer)
    greet(ep=inward)

    @pl.when(zz == 1)
    def _():
        greet(ep=outward)

    own = held.at[me, sec]
    own[:width, :] = tokens[...]
    own[width : 2 * width, :] = grad_out[...]
    n_ep = held.shape[0]
    expert = lax.broadcasted_iota(jnp.int32, (n_ep, n_tok), 0)
    weight = jnp.zeros((n_ep, n_tok), jnp.float32)
    for k in range(ids.shape[0]):
        weight = weight + jnp.where(ids[k : k + 1, :] == expert, probs[k : k + 1, :], 0.0)
    high = weight.astype(jnp.bfloat16).astype(jnp.float32)
    own[2 * width :, :] = jnp.concatenate([high, weight - high], axis=0).astype(jnp.bfloat16)

    @pl.when(zz == 0)
    def _():
        pl.semaphore_wait(barrier, 4)

    @pl.when(zz == 1)
    def _():
        pl.semaphore_wait(barrier, 5)

    def send(block, send_sem, recv_sem, **where):
        return pltpu.make_async_remote_copy(
            src_ref=block, dst_ref=block, send_sem=send_sem, recv_sem=recv_sem,
            device_id=where, device_id_type=MESH,
        )

    def source(k):
        s = k + (1 - k // 2) * ((k + zz) % 2 - k % 2)
        return s + h * (3 - 2 * s)

    def mine(k):
        return 2 * source(k) + y

    def other(k):
        return 2 * source(k) + 1 - y

    def upper(block, first):
        return block.at[pl.ds(0, half)] if first else block.at[pl.ds(along, side)]

    def lower(block, first):
        return block.at[pl.ds(half, half)] if first else block.at[pl.ds(along + side, side)]

    def d_block(k):
        return held.at[other(k), x_peer, pl.ds(0, along)]

    def d_in(k, idx):
        return send(d_block(k), d_send.at[0, idx], d_recv.at[idx], ep=inward)

    def d_out(k, idx):
        return send(d_block(k), d_send.at[1, idx], d_recv.at[idx], ep=outward)

    def d_arrived(k):
        send(d_block(k), d_send.at[0, k], d_recv.at[k], ep=inward).wait_recv()

    def z_arrived(k):
        send(held.at[mine(k), sec], z_send.at[0, k], z_recv.at[k], ep=inward).wait_recv()

    def z_in(k, idx):
        return send(held.at[mine(k), sec], z_send.at[0, idx], z_recv.at[idx], ep=inward)

    def z_out(k, idx):
        return send(held.at[mine(k), sec], z_send.at[1, idx], z_recv.at[idx], ep=outward)

    def x_whole(k):
        return send(held.at[mine(k), sec], x_send.at[k], x_recv.at[k], section=x_peer)

    def y_whole(k):
        return send(held.at[mine(k), sec], y_send.at[k], y_recv.at[k], ep=y_peer)

    def x_half(k, first):
        return send(upper(held.at[other(k), sec], first), dx_send.at[k], dx_recv.at[k], section=x_peer)

    def y_half(k, first):
        return send(lower(held.at[mine(k), x_peer], first), dy_send.at[k], dy_recv.at[k], ep=y_peer)

    def by_step(k, act):
        @pl.when(k == 0)
        def _():
            act(True)

        @pl.when(k > 0)
        def _():
            act(False)

    def core(k, which):
        block = held.at[mine(k) if which < 2 else other(k), sec if which % 2 == 0 else x_peer]
        return send(block, c_send.at[k, which], c_recv.at[k, which], section=core_peer)

    def x_arrived(k):
        send(held.at[mine(k), x_peer], x_send.at[k], x_recv.at[k], section=x_peer).wait_recv()

    def y_arrived(k):
        send(held.at[other(k), sec], y_send.at[k], y_recv.at[k], ep=y_peer).wait_recv()

    def diagonal_arrived(k):
        block = held.at[other(k), x_peer]

        def sides(first):
            send(upper(block, first), dx_send.at[k], dx_recv.at[k], section=x_peer).wait_recv()
            send(lower(block, first), dy_send.at[k], dy_recv.at[k], ep=y_peer).wait_recv()

        by_step(k, sides)

        @pl.when((zz == 0) & (k > 0))
        def _():
            d_arrived(k)

    def core_arrived(k, which):
        block = held.at[
            mine(k) if which < 2 else other(k),
            core_peer if which % 2 == 0 else (core_peer + 2) % 4,
        ]
        send(block, c_send.at[k, which], c_recv.at[k, which], section=core_peer).wait_recv()

    def column(k):
        x_whole(k).start()
        y_whole(k).start()
        core(k, 0).start()

    def forward(slot, start):
        here = pl.ds(start, n_tok)
        block = held.at[slot]
        parts = block[0, 2 * width :, :].astype(jnp.float32)
        which = lax.broadcasted_iota(jnp.int32, parts.shape, 0) % n_ep
        weight = jnp.sum(jnp.where(which == me, parts, 0.0), axis=0, keepdims=True)
        for s in range(n_sec):
            part = pl.ds(s * width, width)
            cols_in[part, here] = block[s, :width, :]
            cot = block[s, width : 2 * width, :].astype(jnp.float32)
            cols_scaled[part, here] = (weight * cot).astype(jnp.bfloat16)
        for at in range(0, units, units // 3):
            part = pl.ds(at, units // 3)
            gate = jnp.dot(wg_t[part, :], cols_in[:, here], preferred_element_type=jnp.float32)
            linear = jnp.dot(wu_t[part, :], cols_in[:, here], preferred_element_type=jnp.float32)
            grad = jnp.dot(wd[part, :], cols_scaled[:, here], preferred_element_type=jnp.float32)
            sigma = jax.nn.sigmoid(gate)
            silu = gate * sigma
            term_hidden[part, here] = (silu * linear).astype(jnp.bfloat16)
            term_gate[part, here] = (grad * linear * sigma * (1.0 + gate * (1.0 - sigma))).astype(jnp.bfloat16)
            term_linear[part, here] = (grad * silu).astype(jnp.bfloat16)

    def outer(lhs, rhs):
        return lax.dot_general(lhs, rhs, (((1,), (1,)), ((), ())), preferred_element_type=jnp.float32)

    products = (
        (acc_gate, part_gate, cols_in, term_gate, units),
        (acc_up, part_up, cols_in, term_linear, units),
        (acc_down, part_down, term_hidden, cols_scaled, feats),
    )

    def first_weights():
        for acc, _, lhs, rhs, size in products:
            for at in range(0, size, TILE):
                to = min(size, at + TILE)
                acc[:, at:to] = outer(lhs[...], rhs[at:to, :])

    def second_weights():
        both = 2 * n_tok
        for acc, part, lhs, rhs, size in products:
            for at in range(0, size, TILE):
                to = min(size, at + TILE)
                part[:, at:to] = (acc[:, at:to] + outer(lhs[:, :both], rhs[at:to, :both])).astype(jnp.bfloat16)

    z_in(0, 1 + zz).start()

    @pl.when(zz == 1)
    def _():
        z_out(0, 1).start()

    column(0)

    for load in loads:
        load.wait()
    for at in range(0, feats, TILE):
        to = min(feats, at + TILE)
        wg_t[:, at:to] = wg[at:to, :].T
        wu_t[:, at:to] = wu[at:to, :].T

    pairs = (
        (part_gate, out_gate), (part_up, out_up), (part_down, out_down), (cols_in, out_in), (cols_scaled, out_scaled),
        (term_gate, out_term_gate), (term_linear, out_term_linear), (term_hidden, out_term_hidden),
    )
    results = [pltpu.make_async_copy(src, dst, out_sem.at[i]) for i, (src, dst) in enumerate(pairs)]

    def step(k, carry):
        x_arrived(k)
        by_step(k, lambda first: y_half(k, first).start())
        core(k, 1).start()
        y_arrived(k)
        by_step(k, lambda first: x_half(k, first).start())
        core(k, 2).start()

        @pl.when(k == 0)
        def _():
            z_arrived(1)

            @pl.when(zz == 1)
            def _():
                z_in(1, 3).start()
                z_arrived(2)
                z_out(2, 2).start()

            column(1)

        core_arrived(k, 0)
        core_arrived(k, 1)
        forward(mine(k), pl.multiple_of((1 - (k + 3) // 4) * 2 * n_tok, n_tok))

        @pl.when(k == 0)
        def _():
            diagonal_arrived(0)
            core(0, 3).start()
            d_in(0, 1 + zz).start()

            @pl.when(zz == 1)
            def _():
                d_out(0, 1).start()
                z_arrived(3)
                z_out(3, 3).start()

            @pl.when(zz == 0)
            def _():
                z_arrived(2)

            column(2)

        @pl.when((zz == 1) & (k == 1))
        def _():
            d_arrived(1)
            d_in(1, 3).start()
            d_arrived(2)
            d_out(2, 2).start()

        @pl.when(k > 0)
        def _():
            core_arrived(k - 1, 2)
            core_arrived(k - 1, 3)
            forward(other(k - 1), n_tok)

        @pl.when(k == 1)
        def _():
            @pl.when(zz == 0)
            def _():
                z_arrived(3)

            column(3)
            first_weights()

            @pl.when(zz == 1)
            def _():
                d_arrived(3)
                d_out(3, 3).start()

        @pl.when(k == 2)
        def _():
            second_weights()
            for result in results[:3]:
                result.start()

        @pl.when(k > 0)
        def _():
            diagonal_arrived(k)
            core(k, 3).start()

        return carry

    lax.fori_loop(0, 4, step, 0)
    core_arrived(3, 2)
    core_arrived(3, 3)
    forward(other(3), 2 * n_tok)

    for result in results[3:]:
        result.start()
    z_in(0, 1 + zz).wait_send()
    d_in(0, 1 + zz).wait_send()

    @pl.when(zz == 1)
    def _():
        z_out(0, 1).wait_send()
        z_in(1, 3).wait_send()
        z_out(2, 2).wait_send()
        z_out(3, 3).wait_send()
        d_out(0, 1).wait_send()
        d_in(1, 3).wait_send()
        d_out(2, 2).wait_send()
        d_out(3, 3).wait_send()

    def drain(k, carry):
        x_whole(k).wait_send()
        y_whole(k).wait_send()

        def sides(first):
            x_half(k, first).wait_send()
            y_half(k, first).wait_send()

        by_step(k, sides)
        for which in range(4):
            core(k, which).wait_send()
        return carry

    lax.fori_loop(0, 4, drain, 0)
    for result in results:
        result.wait()


def last_kernel(
    part_gate, part_up, part_down, cols_in, cols_scaled, term_gate, term_linear, term_hidden, out_gate, out_up, out_down
):
    def outer(lhs, rhs):
        return lax.dot_general(lhs, rhs, (((1,), (1,)), ((), ())), preferred_element_type=jnp.float32)

    for part, out, lhs, rhs in (
        (part_gate, out_gate, cols_in, term_gate),
        (part_up, out_up, cols_in, term_linear),
        (part_down, out_down, term_hidden, cols_scaled),
    ):
        out[...] = (part[...].astype(jnp.float32) + outer(lhs[...], rhs[...])).astype(jnp.bfloat16)


def fused(tokens, grad_out, expert_ids, probs, w_gate, w_up, w_down):
    n_ep, n_sec = lax.axis_size("ep"), lax.axis_size("section")
    n_tok, width = tokens.shape
    feats, units = w_gate.shape[1:]
    bf16, f32 = jnp.bfloat16, jnp.float32
    dma = pltpu.SemaphoreType.DMA
    vmem, hbm = pl.BlockSpec(memory_space=pltpu.VMEM), pl.BlockSpec(memory_space=pl.ANY)
    rows = n_ep * n_tok
    shapes = (
        jax.ShapeDtypeStruct((feats, units), bf16),
        jax.ShapeDtypeStruct((feats, units), bf16),
        jax.ShapeDtypeStruct((units, feats), bf16),
    )
    outs = pl.pallas_call(
        fused_kernel,
        out_shape=shapes
        + tuple(jax.ShapeDtypeStruct((size, 3 * n_tok), bf16) for size in (feats, feats, units, units, units)),
        in_specs=[vmem] * 4 + [hbm] * 3,
        out_specs=(hbm,) * 8,
        scratch_shapes=[
            pltpu.VMEM((n_ep, n_sec, 2 * width + 2 * n_ep, n_tok), bf16),
            pltpu.VMEM((feats, units), bf16),
            pltpu.VMEM((feats, units), bf16),
            pltpu.VMEM((units, feats), bf16),
            pltpu.VMEM((units, feats), bf16),
            pltpu.VMEM((units, feats), bf16),
            pltpu.VMEM((feats, units), f32),
            pltpu.VMEM((feats, units), f32),
            pltpu.VMEM((units, feats), f32),
            pltpu.VMEM((feats, 3 * n_tok), bf16),
            pltpu.VMEM((feats, 3 * n_tok), bf16),
            pltpu.VMEM((units, 3 * n_tok), bf16),
            pltpu.VMEM((units, 3 * n_tok), bf16),
            pltpu.VMEM((units, 3 * n_tok), bf16),
            pltpu.VMEM((feats, units), bf16),
            pltpu.VMEM((feats, units), bf16),
            pltpu.VMEM((units, feats), bf16),
            dma((8,)),
            dma((3,)),
            dma((2, 4)), dma((4,)),
            dma((4,)), dma((4,)), dma((4,)), dma((4,)),
            dma((4,)), dma((4,)), dma((4,)), dma((4,)),
            dma((4, 4)), dma((4, 4)),
            dma((2, 4)), dma((4,)),
        ],
        cost_estimate=pl.CostEstimate(
            flops=12 * rows * feats * units, bytes_accessed=12 * feats * units, transcendentals=rows * units
        ),
        compiler_params=pltpu.CompilerParams(
            collective_id=0, has_side_effects=True, vmem_limit_bytes=60 * 1024 * 1024
        ),
    )(tokens.T, grad_out.T, expert_ids.T, probs.T, w_gate[0], w_up[0], w_down[0])
    steps = 5

    def by_rows(size, other):
        return pl.BlockSpec((size // steps, other), lambda i: (i, 0))

    def whole(size):
        return pl.BlockSpec((size, 3 * n_tok), lambda i: (0, 0))

    blocks = [by_rows(feats, units), by_rows(feats, units), by_rows(units, feats)]
    outs = pl.pallas_call(
        last_kernel,
        out_shape=shapes,
        grid=(steps,),
        in_specs=blocks
        + [by_rows(feats, 3 * n_tok), whole(feats), whole(units), whole(units), by_rows(units, 3 * n_tok)],
        out_specs=tuple(blocks),
        cost_estimate=pl.CostEstimate(
            flops=18 * n_tok * feats * units, bytes_accessed=12 * feats * units, transcendentals=0
        ),
        compiler_params=pltpu.CompilerParams(vmem_limit_bytes=60 * 1024 * 1024),
    )(*outs)
    return tuple(out[None] for out in outs)


def solution(mesh):
    body = shards
    if mesh.shape["ep"] == 8 and mesh.shape["section"] == 4:
        body = fused
    placed = (
        P("ep", "section"),
        P("ep", "section"),
        P("ep", None),
        P("ep", None),
        P("ep", None, "section"),
        P("ep", None, "section"),
        P("ep", "section", None),
    )
    return jax.shard_map(
        body,
        mesh=mesh,
        in_specs=placed,
        out_specs=(P("ep", None, "section"), P("ep", None, "section"), P("ep", "section", None)),
        check_vma=False,
    )
```
